512 devices in a mesh: dp: 64 (over z, y_hi, core), mp: 8 (over x, y_lo).
Axes of the slice: x: 4, y: 4 (y_hi: 2, y_lo: 2; y = y_hi * 2 + y_lo), z: 16, core: 2. Of those that a mesh axis runs over, the one named last changes fastest.
Arguments:
- acts: bfloat16 [32768, 8192], P('dp', 'mp'), may hold values from -6 to 6
- out_grads: bfloat16 [32768, 14336], P('dp', 'mp'), may hold values from -0.09375 to 0.09375
- basis: bfloat16 [8192, 512], P('mp'), may hold values from -0.0625 to 0.0625
- weights: bfloat16 [14336, 8192], P(('mp', 'dp')), may hold values from -0.59765625 to 0.59765625
- first_moment: float32 [14336, 512], P(('mp', 'dp')), may hold values from -2 to 2
- second_moment: float32 [14336, 512], P(('mp', 'dp')), may hold values from 0.05 to 1
Outputs:
- new_weights: bfloat16 [14336, 8192], P(('mp', 'dp'))
- moment_new: float32 [14336, 512], P(('mp', 'dp'))
- second_new: float32 [14336, 512], P(('mp', 'dp'))
The draws below stay inside these ranges and needn't reach their ends.
All inputs are finite; a program needn't handle non-finite values.
Results may differ from the reference program's by a relative error of at most 0.01.
Values may be sent and summed in bfloat16 or wider, within the bound.
A program may use at most 64 MiB of HBM per device.

```python
import math
import jax
import jax.numpy as jnp
from jax import lax

D = 8192
FFW = 14336
RANK = 512
TOKENS = 32768


def strengthened(entries, stream_key, source, target, parts, factor):
    def block_of(axis_at):
        return (jnp.arange(entries.shape[axis_at]) // (entries.shape[axis_at] // parts)).reshape((-1,) + (1,) * (entries.ndim - 1 - axis_at))

    first = jax.random.permutation(stream_key, parts)[block_of(target)]
    far = (block_of(target) + parts // 2) % parts
    return jnp.where((block_of(source) == first) | (block_of(source) == far), factor * entries, entries)


def levels(stream_key, shape, shards, least, top_value):
    level = 1.0
    for position, parts in shards:
        draws = jax.random.uniform(jax.random.fold_in(jax.random.fold_in(stream_key, 6), position), (parts,), jnp.float32, least / len(shards), top_value / len(shards))
        level = level * jnp.repeat(jnp.exp(draws), shape[position] // parts).reshape((-1,) + (1,) * (len(shape) - 1 - position))
    return level


def gaussian(stream_key, extent, spread, limit, cuts=(), kind=jnp.bfloat16):
    result = jax.random.normal(stream_key, extent, jnp.float32) * spread
    if len(cuts) > 0:
        result = levels(stream_key, extent, cuts, -0.22, 0.18) * result
    return jnp.clip(result, min=-limit, max=limit).astype(kind)


def gaussian_with(own_key, dims, deviation, limit, pieces, heavy, kind=jnp.bfloat16):
    drawn = deviation * jax.random.normal(own_key, dims, jnp.float32)
    if pieces:
        drawn = drawn * levels(own_key, dims, pieces, -0.22, 0.18)
    return jnp.clip(strengthened(drawn, jax.random.fold_in(own_key, 3), *heavy), -limit, limit).astype(kind)


def setup_inputs(seed: int = 0) -> dict:
    keys = jax.random.split(jax.random.key(seed), 7)
    return {
        "acts": gaussian(keys[0], (TOKENS, D), 1.0, 6.0, ((0, 64), (1, 8))),
        "out_grads": gaussian_with(keys[1], (TOKENS, FFW), TOKENS ** -0.5, 0.09375, ((0, 64), (1, 8)), (0, 1, 64, 4.0)),
        "basis": gaussian(keys[2], (D, RANK), D ** -0.5, 0.0625, ((0, 8),)),
        "weights": gaussian(keys[3], (FFW, D), 0.1, 0.59765625, ((0, 512),)),
        "first_moment": gaussian(keys[4], (FFW, RANK), 0.3, 2.0, ((0, 512),), jnp.float32),
        "second_moment": jnp.clip(jnp.exp(math.log(1.0) - 2.9957323 * jax.random.uniform(keys[5], (FFW, RANK), jnp.float32) ** levels(keys[5], (FFW, RANK), ((0, 512),), -0.2, 0.2)), 0.05, 1.0),
    }


beta_one = 0.9
beta_two = 0.99
corr_one = 1.0 - 0.9 ** 10
corr_two = 1.0 - 0.99 ** 10
adam_eps = 1e-08
step_size = 1.0

def reference(acts, out_grads, basis, weights, first_moment, second_moment):
    projected = jnp.dot(acts, basis, preferred_element_type=jnp.float32).astype(jnp.bfloat16)
    low_grad = lax.dot_general(out_grads, projected, (((0,), (0,)), ((), ())), preferred_element_type=jnp.float32)
    moment_new = beta_one * first_moment + (1.0 - beta_one) * low_grad
    second_new = beta_two * second_moment + (1.0 - beta_two) * low_grad * low_grad
    direction = (moment_new / corr_one / (jnp.sqrt(second_new / corr_two) + adam_eps)).astype(jnp.bfloat16)
    delta = lax.dot_general(direction, basis, (((1,), (1,)), ((), ())), preferred_element_type=jnp.float32)
    new_weights = (weights.astype(jnp.float32) - step_size * delta).astype(jnp.bfloat16)
    return (new_weights, moment_new, second_new)
```

```python
import functools

import jax
import jax.numpy as jnp
from jax import lax
from jax.experimental import pallas as pl
from jax.experimental.pallas import tpu as pltpu
from jax.sharding import PartitionSpec as P

beta_one = 0.9
beta_two = 0.99
corr_one = 1.0 - 0.9**10
corr_two = 1.0 - 0.99**10
adam_eps = 1e-08
step_size = 1.0

MESH = pl.DeviceIdType.MESH
F32 = jnp.float32
BF16 = jnp.bfloat16


def kernel(
    nz, nx, pad,
    acts_hbm, grads_hbm, basis_hbm, weights_hbm, first_hbm, second_hbm,
    weights_out, first_out, second_out,
    acts, grads, basis, weights, first, second,
    part, part_in, proj, turned,
    quarters, sibling_in, down_out, down_in, up_out, up_in,
    column, fin_out, fin_in, dirs, blocks, delta,
    load_sem, rs_send, rs_recv, ag_send, ag_recv, core_send, core_recv,
    down_send, down_recv, up_send, up_recv, fin_send, fin_recv,
    dir_send, dir_recv, blk_send, blk_recv,
):
    dp, mp = lax.axis_index("dp"), lax.axis_index("mp")
    z, y_hi, core = dp // 4, (dp // 2) % 2, dp % 2
    x, y_lo = mp // 2, mp % 2
    tokens, width = acts.shape
    hidden = turned.shape[0]
    rank = basis.shape[1]
    rows = first.shape[0]
    span = hidden // nz
    piece = tokens // (2 * nx)

    def dp_of(z_at, y_at, core_at):
        return (z_at % nz) * 4 + y_at * 2 + core_at

    def mp_of(r, dy):
        return ((x + r + nx) % nx) * 2 + (y_lo + dy) % 2

    loads = [
        pltpu.make_async_copy(src, dst, load_sem.at[i])
        for i, (src, dst) in enumerate(
            (
                (basis_hbm, basis),
                (acts_hbm, acts),
                (grads_hbm, grads),
                (weights_hbm, weights),
                (first_hbm, first),
                (second_hbm, second),
            )
        )
    ]
    for load in loads:
        load.start()

    relations = [(r, dy) for r in range(nx) for dy in range(2)]
    peers = [({"mp": mp_of(r, dy)}) for r, dy in relations[1:]]
    peers += [
        {"dp": dp_of(z, y_hi, 1 - core)},
        {"dp": dp_of(z + nz - 1, y_hi, core)},
        {"dp": dp_of(z + 1, y_hi, core)},
        {"dp": dp_of(z, 1 - y_hi, core)},
        {"dp": dp_of(z, 1 - y_hi, 1 - core)},
    ]
    barrier = pltpu.get_barrier_semaphore()
    for peer in peers:
        pl.semaphore_signal(barrier, inc=1, device_id=peer, device_id_type=MESH)

    def send(src, dst, send_sem, recv_sem, device):
        copy = pltpu.make_async_remote_copy(
            src_ref=src, dst_ref=dst, send_sem=send_sem, recv_sem=recv_sem,
            device_id=device, device_id_type=MESH,
        )
        copy.start()
        return copy

    loads[0].wait()
    loads[1].wait()

    def project(r):
        x_at = (x + r) % nx
        at = pl.multiple_of(x_at * 2 * piece, 2 * piece)
        value = jnp.dot(acts[pl.ds(at, 2 * piece), :], basis[...], preferred_element_type=F32)
        part[pl.ds(at, 2 * piece), :] = value.astype(BF16)

    def piece_of(ref, index):
        return ref.at[pl.ds(pl.multiple_of(index * piece, piece), piece), :]

    order = [nx // 2] + [r for r in range(1, nx) if r != nx // 2] + [0]
    rs = {}
    for n, r in enumerate(order):
        project(r)
        if n == 0:
            pl.semaphore_wait(barrier, len(peers))
        for dy in range(2):
            q = 2 * r + dy
            if q:
                rs[q] = send(
                    piece_of(part, mp_of(r, dy)), part_in.at[q],
                    rs_send.at[q], rs_recv.at[q], {"mp": mp_of(r, dy)},
                )

    loads[2].wait()
    for b in range(hidden // 128):
        turned[pl.ds(b * 128, 128), :] = grads[:, pl.ds(b * 128, 128)].T

    total = part[pl.ds(pl.multiple_of(mp * piece, piece), piece), :].astype(F32)
    for q in range(1, 2 * nx):
        rs[q].wait()
        total = total + part_in[q].astype(F32)
    proj[pl.ds(pl.multiple_of(mp * piece, piece), piece), :] = total.astype(BF16)
    ag = []
    for q, (r, dy) in enumerate(relations):
        if q:
            ag.append(
                send(
                    piece_of(proj, mp), piece_of(proj, mp),
                    ag_send.at[q], ag_recv.at[q], {"mp": mp_of(r, dy)},
                )
            )
    for copy in ag:
        copy.wait()

    half = nz // 2
    schedule = [(-half, "down", 0)]
    for k in range(half - 1):
        schedule.append((-(half - 1 - k), "down", k + 1))
        schedule.append((half - 1 - k, "up", k))
    schedule.append((0, "own", 0))
    siblings = [None] * len(schedule)

    def multiply(n):
        at = (z + schedule[n][0] + nz) % nz
        value = jnp.dot(
            turned[pl.ds(pl.multiple_of(at * span, 16), span), :], proj[...],
            preferred_element_type=F32,
        ).astype(BF16)
        for i in range(4):
            quarters[n, i] = value[:, i * (rank // 4) : (i + 1) * (rank // 4)]
        siblings[n] = send(
            quarters.at[n, pl.ds(2 * (1 - core), 2)], sibling_in.at[n],
            core_send.at[n], core_recv.at[n], {"dp": dp_of(z, y_hi, 1 - core)},
        )

    ring = {}
    ahead = 4
    for n in range(min(ahead, len(schedule))):
        multiply(n)
    for n, (_, way, k) in enumerate(schedule):
        siblings[n].wait()
        for s in range(2):
            value = quarters[n, 2 * core + s].astype(F32) + sibling_in[n, s].astype(F32)
            if way == "own":
                ring["down", half - 1, s].wait()
                ring["up", half - 2, s].wait()
                value = value + down_in[half - 1, s].astype(F32) + up_in[half - 2, s].astype(F32)
                column[pl.ds(0, span), pl.ds(s * 128, 128)] = value
                continue
            out, into, sent, received, towards = (
                (up_out, up_in, up_send, up_recv, z + 1)
                if way == "up"
                else (down_out, down_in, down_send, down_recv, z + nz - 1)
            )
            if k:
                ring[way, k - 1, s].wait()
                value = value + into[k - 1, s].astype(F32)
            out[k, s] = value.astype(BF16)
            ring[way, k, s] = send(
                out.at[k, s], into.at[k, s], sent.at[k, s], received.at[k, s],
                {"dp": dp_of(towards, y_hi, core)},
            )
        if n + ahead < len(schedule):
            multiply(n + ahead)

    column[pl.ds(span, 8), :] = jnp.zeros((8, rank // 2), F32)
    here = y_hi * 2 + core
    for b in range(4):
        for s in range(2):
            fin_out[b, s] = column[pl.ds(b * rows, pad), pl.ds(s * 128, 128)].astype(BF16)
    fin = []
    for i, (dy, dc) in enumerate(((1, 0), (1, 1), (0, 1))):
        y_at, core_at = (y_hi + dy) % 2, (core + dc) % 2
        fin.append(
            send(
                fin_out.at[y_at * 2 + core_at], fin_in.at[here],
                fin_send.at[i], fin_recv.at[i], {"dp": dp_of(z, y_at, core_at)},
            )
        )
    fin_in[here] = fin_out[here]
    for load in loads[3:]:
        load.wait()
    for copy in fin:
        copy.wait()

    for c in range(2):
        for s in range(2):
            low_grad = (fin_in[c, s].astype(F32) + fin_in[2 + c, s].astype(F32))[:rows]
            cut = pl.ds((2 * c + s) * 128, 128)
            moment_new = beta_one * first[:, cut] + (1.0 - beta_one) * low_grad
            second_new = beta_two * second[:, cut] + (1.0 - beta_two) * low_grad * low_grad
            direction = moment_new / corr_one / (jnp.sqrt(second_new / corr_two) + adam_eps)
            first_out[:, cut] = moment_new
            second_out[:, cut] = second_new
            padded = jnp.concatenate([direction, jnp.zeros((pad - rows, 128), F32)], axis=0)
            dirs[0, :, cut] = padded.astype(BF16)

    gathered = {}
    for q, (r, dy) in enumerate(relations):
        if q:
            gathered[q] = send(
                dirs.at[0], dirs.at[q], dir_send.at[q], dir_recv.at[q], {"mp": mp_of(r, dy)},
            )
    for copy in gathered.values():
        copy.wait()
    stacked = dirs[...].reshape(2 * nx * pad, rank)
    product = lax.dot_general(
        stacked, basis[...], (((1,), (1,)), ((), ())), preferred_element_type=F32
    ).astype(BF16)
    returned = {}
    for q, (r, dy) in enumerate(relations):
        if q:
            blocks[q] = product[q * pad : (q + 1) * pad]
            returned[q] = send(
                blocks.at[q], delta.at[q], blk_send.at[q], blk_recv.at[q], {"mp": mp_of(-r, dy)},
            )
        else:
            delta[0] = product[:pad]
    for q, (r, dy) in enumerate(relations):
        if q:
            returned[q].wait()
        at = pl.ds(pl.multiple_of(mp_of(r, dy) * width, width), width)
        change = delta[q].astype(F32)[:rows]
        weights_out[:, at] = (weights[:, at].astype(F32) - step_size * change).astype(BF16)


def on_device(nz, nx, acts, out_grads, basis, weights, first_moment, second_moment):
    tokens, width = acts.shape
    hidden = out_grads.shape[1]
    rank = basis.shape[1]
    rows, full = weights.shape
    pad = -(-rows // 16) * 16
    span = hidden // nz
    peers = 2 * nx
    piece = tokens // peers
    half = nz // 2
    dma = pltpu.SemaphoreType.DMA
    vmem = pltpu.VMEM
    return pl.pallas_call(
        functools.partial(kernel, nz, nx, pad),
        out_shape=(
            jax.ShapeDtypeStruct(weights.shape, BF16),
            jax.ShapeDtypeStruct(first_moment.shape, F32),
            jax.ShapeDtypeStruct(second_moment.shape, F32),
        ),
        in_specs=[pl.BlockSpec(memory_space=pl.ANY)] * 6,
        out_specs=[pl.BlockSpec(memory_space=pltpu.VMEM)] * 3,
        scratch_shapes=[
            vmem(acts.shape, BF16),
            vmem(out_grads.shape, BF16),
            vmem(basis.shape, BF16),
            vmem(weights.shape, BF16),
            vmem(first_moment.shape, F32),
            vmem(second_moment.shape, F32),
            vmem((tokens, rank), BF16),
            vmem((peers, piece, rank), BF16),
            vmem((tokens, rank), BF16),
            vmem((hidden, tokens), BF16),
            vmem((nz, 4, span, rank // 4), BF16),
            vmem((nz, 2, span, rank // 4), BF16),
            vmem((half, 2, span, rank // 4), BF16),
            vmem((half, 2, span, rank // 4), BF16),
            vmem((half, 2, span, rank // 4), BF16),
            vmem((half, 2, span, rank // 4), BF16),
            vmem((span + 8, rank // 2), F32),
            vmem((4, 2, pad, rank // 4), BF16),
            vmem((4, 2, pad, rank // 4), BF16),
            vmem((peers, pad, rank), BF16),
            vmem((peers, pad, width), BF16),
            vmem((peers, pad, width), BF16),
            dma((6,)),
            dma((peers,)), dma((peers,)), dma((peers,)), dma((peers,)),
            dma((nz,)), dma((nz,)),
            dma((half, 2)), dma((half, 2)), dma((half, 2)), dma((half, 2)),
            dma((3,)), dma((3,)),
            dma((peers,)), dma((peers,)), dma((peers,)), dma((peers,)),
        ],
        compiler_params=pltpu.CompilerParams(
            collective_id=0, has_side_effects=True, vmem_limit_bytes=48 * 1024 * 1024
        ),
    )(acts, out_grads, basis, weights, first_moment, second_moment)


def solution(mesh):
    nz, nx = mesh.shape["dp"] // 4, mesh.shape["mp"] // 2
    return jax.shard_map(
        functools.partial(on_device, nz, nx),
        mesh=mesh,
        in_specs=(
            P("dp", "mp"),
            P("dp", "mp"),
            P("mp", None),
            P(("mp", "dp"), None),
            P(("mp", "dp"), None),
            P(("mp", "dp"), None),
        ),
        out_specs=(P(("mp", "dp"), None), P(("mp", "dp"), None), P(("mp", "dp"), None)),
        check_vma=False,
    )
```

```python
import functools

import jax
import jax.numpy as jnp
from jax import lax
from jax.experimental import pallas as pl
from jax.experimental.pallas import tpu as pltpu
from jax.sharding import PartitionSpec as P

beta_one = 0.9
beta_two = 0.99
corr_one = 1.0 - 0.9**10
corr_two = 1.0 - 0.99**10
adam_eps = 1e-08
step_size = 1.0

HUBS = (6, -6, 3, -3, 0)
LEAVES = {6: (8, 7, 5, 6), -6: (-7, -5, -6), 3: (4, 2, 3), -3: (-4, -2, -3), 0: (1, -1, 0)}

MESH = pl.DeviceIdType.MESH
F32 = jnp.float32
BF16 = jnp.bfloat16


def kernel(
    nz, nx, pad,
    acts_hbm, grads_hbm, basis_hbm, weights_hbm, first_hbm, second_hbm,
    weights_out, first_out, second_out,
    acts, grads, basis, weights, first, second,
    part, part_in, proj, turned,
    halves, sibling_in, leaf, hub_in, column, fin_out, fin_in, dirs, blocks, delta,
    load_sem, rs_send, rs_recv, ag_send, ag_recv, core_send, core_recv,
    hub_send, hub_recv, fin_send, fin_recv,
    dir_send, dir_recv, blk_send, blk_recv,
):
    dp, mp = lax.axis_index("dp"), lax.axis_index("mp")
    z, y_hi, core = dp // 4, (dp // 2) % 2, dp % 2
    x, y_lo = mp // 2, mp % 2
    tokens, width = acts.shape
    hidden = turned.shape[0]
    rank = basis.shape[1]
    rows = first.shape[0]
    span = hidden // nz
    piece = tokens // (2 * nx)

    def dp_of(z_at, y_at, core_at):
        return (z_at % nz) * 4 + y_at * 2 + core_at

    def mp_of(r, dy):
        return ((x + r + nx) % nx) * 2 + (y_lo + dy) % 2

    loads = [
        pltpu.make_async_copy(src, dst, load_sem.at[i])
        for i, (src, dst) in enumerate(
            (
                (basis_hbm, basis),
                (acts_hbm, acts),
                (grads_hbm, grads),
                (weights_hbm, weights),
                (first_hbm, first),
                (second_hbm, second),
            )
        )
    ]
    for load in loads:
        load.start()

    relations = [(r, dy) for r in range(nx) for dy in range(2)]
    peers = [({"mp": mp_of(r, dy)}) for r, dy in relations[1:]]
    peers += [{"dp": dp_of(z, y_hi, 1 - core)}, {"dp": dp_of(z, 1 - y_hi, core)}]
    for dz in (-2, -1, 1, 2):
        peers += [{"dp": dp_of(z + dz + nz, y_at, core)} for y_at in range(2)]
    for dz in HUBS[:-1]:
        peers += [{"dp": dp_of(z + dz + nz, y_hi, core_at)} for core_at in range(2)]
    barrier = pltpu.get_barrier_semaphore()
    for peer in peers:
        pl.semaphore_signal(barrier, inc=1, device_id=peer, device_id_type=MESH)

    def send(src, dst, send_sem, recv_sem, device):
        copy = pltpu.make_async_remote_copy(
            src_ref=src, dst_ref=dst, send_sem=send_sem, recv_sem=recv_sem,
            device_id=device, device_id_type=MESH,
        )
        copy.start()
        return copy

    loads[0].wait()
    loads[1].wait()

    def project(r):
        x_at = (x + r) % nx
        at = pl.multiple_of(x_at * 2 * piece, 2 * piece)
        value = jnp.dot(acts[pl.ds(at, 2 * piece), :], basis[...], preferred_element_type=F32)
        part[pl.ds(at, 2 * piece), :] = value.astype(BF16)

    def piece_of(ref, index):
        return ref.at[pl.ds(pl.multiple_of(index * piece, piece), piece), :]

    order = [nx // 2] * (nx > 1) + [r for r in range(1, nx) if r != nx // 2] + [0]
    rs = {}
    for n, r in enumerate(order):
        project(r)
        if n == 0:
            pl.semaphore_wait(barrier, len(peers))
        for dy in range(2):
            q = 2 * r + dy
            if q:
                rs[q] = send(
                    piece_of(part, mp_of(r, dy)), part_in.at[q],
                    rs_send.at[q], rs_recv.at[q], {"mp": mp_of(r, dy)},
                )

    loads[2].wait()
    for b in range(hidden // 128):
        turned[pl.ds(b * 128, 128), :] = grads[:, pl.ds(b * 128, 128)].T

    total = part[pl.ds(pl.multiple_of(mp * piece, piece), piece), :].astype(F32)
    for q in range(1, 2 * nx):
        rs[q].wait()
        total = total + part_in[q].astype(F32)
    proj[pl.ds(pl.multiple_of(mp * piece, piece), piece), :] = total.astype(BF16)
    ag = []
    for q, (r, dy) in enumerate(relations):
        if q:
            ag.append(
                send(
                    piece_of(proj, mp), piece_of(proj, mp),
                    ag_send.at[q], ag_recv.at[q], {"mp": mp_of(r, dy)},
                )
            )
    for copy in ag:
        copy.wait()

    schedule = [(h, o) for h in HUBS for o in LEAVES[h]]
    block = rank // 4
    siblings = [None] * len(schedule)

    def multiply(n):
        at = (z - schedule[n][1] + nz) % nz
        value = jnp.dot(
            turned[pl.ds(pl.multiple_of(at * span, 16), span), :], proj[...],
            preferred_element_type=F32,
        )
        for c in range(2):
            for y in range(2):
                two = [
                    value[y * span // 2 : (y + 1) * span // 2, i * block : (i + 1) * block]
                    for i in (2 * c, 2 * c + 1)
                ]
                halves[n, c, y] = jnp.concatenate(two, axis=0).astype(BF16)
        siblings[n] = send(
            halves.at[n, 1 - core], sibling_in.at[n],
            core_send.at[n], core_recv.at[n], {"dp": dp_of(z, y_hi, 1 - core)},
        )

    def slot(e, dy):
        return (e + 1) * 2 + dy

    to_hub = {}

    def scatter(n):
        h, o = schedule[n]
        e = o - h
        siblings[n].wait()
        for y in range(2):
            value = halves[n, core, y].astype(F32) + sibling_in[n, y].astype(F32)
            leaf[n, y] = value.astype(BF16)
        for dy in (1, 0):
            if e or dy:
                y_at = (y_hi + dy) % 2
                i = HUBS.index(h)
                to_hub[h, e, dy] = send(
                    leaf.at[n, y_at], hub_in.at[i, slot(e, dy)],
                    hub_send.at[i, slot(e, dy)], hub_recv.at[i, slot(e, dy)],
                    {"dp": dp_of(z - e + nz, y_at, core)},
                )

    ahead = 4
    for n in range(ahead):
        multiply(n)
    for n in range(len(schedule)):
        scatter(n)
        if n + ahead < len(schedule):
            multiply(n + ahead)

    for load in loads[3:]:
        load.wait()
    column[pl.ds(span, 8), :] = jnp.zeros((8, block), F32)
    fin = {}
    for i, h in enumerate(HUBS):
        own = schedule.index((h, h))
        value = leaf[own, y_hi].astype(F32)
        for e in [o - h for o in LEAVES[h]]:
            for dy in (0, 1):
                if e or dy:
                    to_hub[h, e, dy].wait()
                    value = value + hub_in[i, slot(e, dy)].astype(F32)
        column[pl.ds(0, span), :] = value
        for c in range(2):
            for k in range(2):
                cut = column[pl.ds(k * span // 2 + c * rows, pad), :]
                fin_out[i, c, pl.ds(k * pad, pad), :] = cut.astype(BF16)
        for dc in (1, 0):
            core_at = (core + dc) % 2
            if h or dc:
                fin[i, dc] = send(
                    fin_out.at[i, core_at], fin_in.at[i, dc],
                    fin_send.at[i, dc], fin_recv.at[i, dc],
                    {"dp": dp_of(z - h + nz, y_hi, core_at)},
                )

    for dc in range(2):
        for i, h in enumerate(HUBS):
            if h or dc:
                fin[i, dc].wait()
        for k in range(2):
            at = pl.ds(k * pad, pad)
            low_grad = (fin_in if dc else fin_out)[len(HUBS) - 1, 1 if dc else core, at, :].astype(F32)
            for i in range(len(HUBS) - 1):
                low_grad = low_grad + fin_in[i, dc, at, :].astype(F32)
            low_grad = low_grad[:rows]
            cut = pl.ds(pl.multiple_of(((core + dc) % 2) * 2 * block + k * block, block), block)
            moment_new = beta_one * first[:, cut] + (1.0 - beta_one) * low_grad
            second_new = beta_two * second[:, cut] + (1.0 - beta_two) * low_grad * low_grad
            direction = moment_new / corr_one / (jnp.sqrt(second_new / corr_two) + adam_eps)
            first_out[:, cut] = moment_new
            second_out[:, cut] = second_new
            padded = jnp.concatenate([direction, jnp.zeros((pad - rows, block), F32)], axis=0)
            dirs[0, :, cut] = padded.astype(BF16)

    gathered, returned = {}, {}
    for r in order:
        for dy in (1, 0):
            q = 2 * r + dy
            if q:
                gathered[q] = send(
                    dirs.at[0], dirs.at[q], dir_send.at[q], dir_recv.at[q], {"mp": mp_of(r, dy)},
                )
    for r in list(order[::-1]):
        for dy in range(2):
            if 2 * r + dy:
                gathered[2 * r + dy].wait()
        stacked = dirs[pl.ds(2 * r, 2)].reshape(2 * pad, rank)
        product = lax.dot_general(
            stacked, basis[...], (((1,), (1,)), ((), ())), preferred_element_type=F32
        ).astype(BF16)
        for dy in range(2):
            q = 2 * r + dy
            blocks[q] = product[dy * pad : (dy + 1) * pad]
            if q:
                returned[q] = send(
                    blocks.at[q], delta.at[q], blk_send.at[q], blk_recv.at[q], {"mp": mp_of(-r, dy)},
                )
    for r in list(order[::-1]):
        for dy in range(2):
            q = 2 * r + dy
            if q:
                returned[q].wait()
            at = pl.ds(pl.multiple_of(mp_of(r, dy) * width, width), width)
            change = (delta if q else blocks)[q].astype(F32)[:rows]
            weights_out[:, at] = (weights[:, at].astype(F32) - step_size * change).astype(BF16)


def on_device(nz, nx, acts, out_grads, basis, weights, first_moment, second_moment):
    tokens, width = acts.shape
    hidden = out_grads.shape[1]
    rank = basis.shape[1]
    rows, full = weights.shape
    pad = -(-rows // 16) * 16
    span = hidden // nz
    peers = 2 * nx
    piece = tokens // peers
    hubs = len(HUBS)
    dma = pltpu.SemaphoreType.DMA
    vmem = pltpu.VMEM
    return pl.pallas_call(
        functools.partial(kernel, nz, nx, pad),
        out_shape=(
            jax.ShapeDtypeStruct(weights.shape, BF16),
            jax.ShapeDtypeStruct(first_moment.shape, F32),
            jax.ShapeDtypeStruct(second_moment.shape, F32),
        ),
        in_specs=[pl.BlockSpec(memory_space=pl.ANY)] * 6,
        out_specs=[pl.BlockSpec(memory_space=pltpu.VMEM)] * 3,
        scratch_shapes=[
            vmem(acts.shape, BF16),
            vmem(out_grads.shape, BF16),
            vmem(basis.shape, BF16),
            vmem(weights.shape, BF16),
            vmem(first_moment.shape, F32),
            vmem(second_moment.shape, F32),
            vmem((tokens, rank), BF16),
            vmem((peers, piece, rank), BF16),
            vmem((tokens, rank), BF16),
            vmem((hidden, tokens), BF16),
            vmem((nz, 2, 2, span, rank // 4), BF16),
            vmem((nz, 2, span, rank // 4), BF16),
            vmem((nz, 2, span, rank // 4), BF16),
            vmem((hubs, 8, span, rank // 4), BF16),
            vmem((span + 8, rank // 4), F32),
            vmem((hubs, 2, 2 * pad, rank // 4), BF16),
            vmem((hubs, 2, 2 * pad, rank // 4), BF16),
            vmem((peers, pad, rank), BF16),
            vmem((peers, pad, width), BF16),
            vmem((peers, pad, width), BF16),
            dma((6,)),
            dma((peers,)), dma((peers,)), dma((peers,)), dma((peers,)),
            dma((nz,)), dma((nz,)),
            dma((hubs, 8)), dma((hubs, 8)), dma((hubs, 2)), dma((hubs, 2)),
            dma((peers,)), dma((peers,)), dma((peers,)), dma((peers,)),
        ],
        compiler_params=pltpu.CompilerParams(
            collective_id=0, has_side_effects=True, vmem_limit_bytes=60 * 1024 * 1024
        ),
    )(acts, out_grads, basis, weights, first_moment, second_moment)


def solution(mesh):
    nz, nx = mesh.shape["dp"] // 4, mesh.shape["mp"] // 2
    return jax.shard_map(
        functools.partial(on_device, nz, nx),
        mesh=mesh,
        in_specs=(
            P("dp", "mp"),
            P("dp", "mp"),
            P("mp", None),
            P(("mp", "dp"), None),
            P(("mp", "dp"), None),
            P(("mp", "dp"), None),
        ),
        out_specs=(P(("mp", "dp"), None), P(("mp", "dp"), None), P(("mp", "dp"), None)),
        check_vma=False,
    )
```

```python
import functools

import jax
import jax.numpy as jnp
from jax import lax
from jax.experimental import pallas as pl
from jax.experimental.pallas import tpu as pltpu
from jax.sharding import PartitionSpec as P

beta_one = 0.9
beta_two = 0.99
corr_one = 1.0 - 0.9**10
corr_two = 1.0 - 0.99**10
adam_eps = 1e-08
step_size = 1.0

HUBS = (6, -6, 3, -3, 0)
LEAVES = {6: (8, 7, 5, 6), -6: (-7, -5, -6), 3: (4, 2, 3), -3: (-4, -2, -3), 0: (1, -1, 0)}

MESH = pl.DeviceIdType.MESH
F32 = jnp.float32
BF16 = jnp.bfloat16


def kernel(
    nz, nx, pad,
    acts_hbm, grads_hbm, basis_hbm, weights_hbm, first_hbm, second_hbm,
    weights_out, first_out, second_out,
    acts, grads, basis, weights, first, second,
    part, part_in, proj, turned,
    halves, sibling_in, leaf, hub_in, column, fin_out, fin_in, dirs, blocks, delta,
    load_sem, rs_send, rs_recv, ag_send, ag_recv, core_send, core_recv,
    hub_send, hub_recv, fin_send, fin_recv,
    dir_send, dir_recv, blk_send, blk_recv, relay_sem,
):
    dp, mp = lax.axis_index("dp"), lax.axis_index("mp")
    z, y_hi, core = dp // 4, (dp // 2) % 2, dp % 2
    x, y_lo = mp // 2, mp % 2
    tokens, width = acts.shape
    hidden = turned.shape[0]
    rank = basis.shape[1]
    rows = first.shape[0]
    span = hidden // nz
    piece = tokens // (2 * nx)

    def dp_of(z_at, y_at, core_at):
        return (z_at % nz) * 4 + y_at * 2 + core_at

    def mp_of(r, dy):
        return ((x + r + nx) % nx) * 2 + (y_lo + dy) % 2

    loads = [
        pltpu.make_async_copy(src, dst, load_sem.at[i])
        for i, (src, dst) in enumerate(
            (
                (basis_hbm, basis),
                (acts_hbm, acts),
                (grads_hbm, grads),
                (weights_hbm, weights),
                (first_hbm, first),
                (second_hbm, second),
            )
        )
    ]
    for load in loads:
        load.start()

    relations = [(r, dy) for r in range(nx) for dy in range(2)]
    peers = [({"mp": mp_of(r, dy)}) for r, dy in relations[1:]]
    peers += [
        {"dp": dp_of(z, y_hi, 1 - core)},
        {"dp": dp_of(z, 1 - y_hi, core)},
        {"dp": dp_of(z + 1, y_hi, core)},
        {"dp": dp_of(z + nz - 1, y_hi, core)},
    ]
    barrier = pltpu.get_barrier_semaphore()
    for peer in peers:
        pl.semaphore_signal(barrier, inc=1, device_id=peer, device_id_type=MESH)

    def tell(n):
        for i, dz in enumerate((n, -n)):
            pl.semaphore_signal(
                relay_sem.at[n - 1, i], inc=1,
                device_id={"dp": dp_of(z + dz + nz, y_hi, core)}, device_id_type=MESH,
            )

    def hear(n):
        for i in range(2):
            pl.semaphore_wait(relay_sem.at[n - 1, i], 1)

    def send(src, dst, send_sem, recv_sem, device):
        copy = pltpu.make_async_remote_copy(
            src_ref=src, dst_ref=dst, send_sem=send_sem, recv_sem=recv_sem,
            device_id=device, device_id_type=MESH,
        )
        copy.start()
        return copy

    loads[0].wait()
    loads[1].wait()

    half = rank // 2

    def project(s, r):
        at = pl.ds(pl.multiple_of(((x + r) % nx) * 2 * piece, 2 * piece), 2 * piece)
        value = jnp.dot(
            acts[at, :], basis[:, s * half : (s + 1) * half], preferred_element_type=F32
        )
        part[s, at, :] = value.astype(BF16)

    def piece_of(index):
        return pl.ds(pl.multiple_of(index * piece, piece), piece)

    order = [nx // 2] * (nx > 1) + [r for r in range(1, nx) if r != nx // 2] + [0]
    rs = {}
    for s in range(2):
        for r in order:
            project(s, r)
            if s == 0 and r == order[0]:
                pl.semaphore_wait(barrier, len(peers))
                tell(1)
            for dy in (1, 0):
                q = 2 * r + dy
                if q:
                    rs[s, q] = send(
                        part.at[s, piece_of(mp_of(r, dy)), :], part_in.at[s, q],
                        rs_send.at[s, q], rs_recv.at[s, q], {"mp": mp_of(r, dy)},
                    )

    loads[2].wait()
    for b in range(hidden // 128):
        turned[pl.ds(b * 128, 128), :] = grads[:, pl.ds(b * 128, 128)].T
    hear(1)
    tell(2)

    ag = {}
    for s in range(2):
        total = part[s, piece_of(mp), :].astype(F32)
        for q in range(1, 2 * nx):
            rs[s, q].wait()
            total = total + part_in[s, q].astype(F32)
        proj[s, piece_of(mp), :] = total.astype(BF16)
        for r in order:
            for dy in (1, 0):
                q = 2 * r + dy
                if q:
                    ag[s, q] = send(
                        proj.at[s, piece_of(mp), :], proj.at[s, piece_of(mp), :],
                        ag_send.at[s, q], ag_recv.at[s, q], {"mp": mp_of(r, dy)},
                    )
    hear(2)
    tell(3)

    schedule = [(h, o) for h in HUBS for o in LEAVES[h]]
    block = rank // 4
    siblings, to_hub = {}, {}

    def multiply(s, n):
        at = (z - schedule[n][1] + nz) % nz
        value = jnp.dot(
            turned[pl.ds(pl.multiple_of(at * span, 16), span), :], proj[s],
            preferred_element_type=F32,
        ).reshape(2, span // 2, half)
        for c in range(2):
            halves[s, n, c] = value[:, :, c * block : (c + 1) * block].astype(BF16)
        siblings[s, n] = send(
            halves.at[s, n, 1 - core], sibling_in.at[s, n],
            core_send.at[s, n], core_recv.at[s, n], {"dp": dp_of(z, y_hi, 1 - core)},
        )

    def slot(e, dy):
        return (e + 1) * 2 + dy

    def scatter(s, n):
        h, o = schedule[n]
        e = o - h
        i = HUBS.index(h)
        siblings[s, n].wait()
        value = halves[s, n, core].astype(F32) + sibling_in[s, n].astype(F32)
        leaf[s, n] = value.astype(BF16)
        for dy in (1, 0):
            if e or dy:
                y_at = (y_hi + dy) % 2
                to_hub[s, h, e, dy] = send(
                    leaf.at[s, n, y_at], hub_in.at[s, i, slot(e, dy)],
                    hub_send.at[s, i, slot(e, dy)], hub_recv.at[s, i, slot(e, dy)],
                    {"dp": dp_of(z - e + nz, y_at, core)},
                )

    ahead = 4
    for s in range(2):
        for q in range(1, 2 * nx):
            ag[s, q].wait()
        for n in range(ahead):
            multiply(s, n)
        for n in range(len(schedule)):
            scatter(s, n)
            if n + ahead < len(schedule):
                multiply(s, n + ahead)
    hear(3)

    for load in loads[3:]:
        load.wait()
    column[:, pl.ds(span // 2, 8), :] = jnp.zeros((2, 8, block), F32)
    fin = {}
    for i, h in enumerate(HUBS):
        own = schedule.index((h, h))
        for s in range(2):
            value = leaf[s, own, y_hi].astype(F32)
            for e in [o - h for o in LEAVES[h]]:
                for dy in (0, 1):
                    if e or dy:
                        to_hub[s, h, e, dy].wait()
                        value = value + hub_in[s, i, slot(e, dy)].astype(F32)
            column[s, pl.ds(0, span // 2), :] = value
            for c in range(2):
                cut = column[s, pl.ds(c * rows, pad), :]
                fin_out[i, c, pl.ds(s * pad, pad), :] = cut.astype(BF16)
        for dc in (1, 0):
            core_at = (core + dc) % 2
            if h or dc:
                fin[i, dc] = send(
                    fin_out.at[i, core_at], fin_in.at[i, dc],
                    fin_send.at[i, dc], fin_recv.at[i, dc],
                    {"dp": dp_of(z - h + nz, y_hi, core_at)},
                )

    for dc in range(2):
        for i, h in enumerate(HUBS):
            if h or dc:
                fin[i, dc].wait()
        for k in range(2):
            at = pl.ds(k * pad, pad)
            low_grad = (fin_in if dc else fin_out)[len(HUBS) - 1, 1 if dc else core, at, :].astype(F32)
            for i in range(len(HUBS) - 1):
                low_grad = low_grad + fin_in[i, dc, at, :].astype(F32)
            low_grad = low_grad[:rows]
            cut = pl.ds(pl.multiple_of((2 * k + (core + dc) % 2) * block, block), block)
            moment_new = beta_one * first[:, cut] + (1.0 - beta_one) * low_grad
            second_new = beta_two * second[:, cut] + (1.0 - beta_two) * low_grad * low_grad
            direction = moment_new / corr_one / (jnp.sqrt(second_new / corr_two) + adam_eps)
            first_out[:, cut] = moment_new
            second_out[:, cut] = second_new
            padded = jnp.concatenate([direction, jnp.zeros((pad - rows, block), F32)], axis=0)
            dirs[0, :, cut] = padded.astype(BF16)

    gathered, returned = {}, {}
    for r in order:
        for dy in (1, 0):
            q = 2 * r + dy
            if q:
                gathered[q] = send(
                    dirs.at[0], dirs.at[q], dir_send.at[q], dir_recv.at[q], {"mp": mp_of(r, dy)},
                )
    for r in list(order[::-1]):
        for dy in range(2):
            if 2 * r + dy:
                gathered[2 * r + dy].wait()
        stacked = dirs[pl.ds(2 * r, 2)].reshape(2 * pad, rank)
        product = lax.dot_general(
            stacked, basis[...], (((1,), (1,)), ((), ())), preferred_element_type=F32
        ).astype(BF16)
        for dy in range(2):
            q = 2 * r + dy
            blocks[q] = product[dy * pad : (dy + 1) * pad]
            if q:
                returned[q] = send(
                    blocks.at[q], delta.at[q], blk_send.at[q], blk_recv.at[q], {"mp": mp_of(-r, dy)},
                )
    for r in list(order[::-1]):
        for dy in range(2):
            q = 2 * r + dy
            if q:
                returned[q].wait()
            at = pl.ds(pl.multiple_of(mp_of(r, dy) * width, width), width)
            change = (delta if q else blocks)[q].astype(F32)[:rows]
            weights_out[:, at] = (weights[:, at].astype(F32) - step_size * change).astype(BF16)


def hand_over(*refs):
    copies = [pltpu.make_async_copy(refs[i], refs[3 + i], refs[6].at[i]) for i in range(3)]
    for copy in copies:
        copy.start()
    for copy in copies:
        copy.wait()


def on_device(nz, nx, acts, out_grads, basis, weights, first_moment, second_moment):
    tokens, width = acts.shape
    hidden = out_grads.shape[1]
    rank = basis.shape[1]
    rows, full = weights.shape
    pad = -(-rows // 16) * 16
    span = hidden // nz
    peers = 2 * nx
    piece = tokens // peers
    hubs = len(HUBS)
    arrays = (acts, out_grads, basis, weights, first_moment, second_moment)
    held = [pltpu.with_memory_space_constraint(array, pltpu.HBM) for array in arrays]
    dma = pltpu.SemaphoreType.DMA
    vmem = pltpu.VMEM
    results = pl.pallas_call(
        functools.partial(kernel, nz, nx, pad),
        out_shape=(
            jax.ShapeDtypeStruct(weights.shape, BF16),
            jax.ShapeDtypeStruct(first_moment.shape, F32),
            jax.ShapeDtypeStruct(second_moment.shape, F32),
        ),
        in_specs=[pl.BlockSpec(memory_space=pltpu.HBM)] * 6,
        out_specs=[pl.BlockSpec(memory_space=pltpu.VMEM)] * 3,
        scratch_shapes=[
            vmem(acts.shape, BF16),
            vmem(out_grads.shape, BF16),
            vmem(basis.shape, BF16),
            vmem(weights.shape, BF16),
            vmem(first_moment.shape, F32),
            vmem(second_moment.shape, F32),
            vmem((2, tokens, rank // 2), BF16),
            vmem((2, peers, piece, rank // 2), BF16),
            vmem((2, tokens, rank // 2), BF16),
            vmem((hidden, tokens), BF16),
            vmem((2, nz, 2, 2, span // 2, rank // 4), BF16),
            vmem((2, nz, 2, span // 2, rank // 4), BF16),
            vmem((2, nz, 2, span // 2, rank // 4), BF16),
            vmem((2, hubs, 8, span // 2, rank // 4), BF16),
            vmem((2, span // 2 + 8, rank // 4), F32),
            vmem((hubs, 2, 2 * pad, rank // 4), BF16),
            vmem((hubs, 2, 2 * pad, rank // 4), BF16),
            vmem((peers, pad, rank), BF16),
            vmem((peers, pad, width), BF16),
            vmem((peers, pad, width), BF16),
            dma((6,)),
            dma((2, peers)), dma((2, peers)), dma((2, peers)), dma((2, peers)),
            dma((2, nz)), dma((2, nz)),
            dma((2, hubs, 8)), dma((2, hubs, 8)), dma((hubs, 2)), dma((hubs, 2)),
            dma((peers,)), dma((peers,)), dma((peers,)), dma((peers,)),
            pltpu.SemaphoreType.REGULAR((3, 2)),
        ],
        compiler_params=pltpu.CompilerParams(
            collective_id=0, has_side_effects=True, vmem_limit_bytes=32 * 1024 * 1024
        ),
    )(*held)
    return pl.pallas_call(
        hand_over,
        out_shape=tuple(jax.ShapeDtypeStruct(r.shape, r.dtype) for r in results),
        in_specs=[pl.BlockSpec(memory_space=pl.ANY)] * 3,
        out_specs=[pl.BlockSpec(memory_space=pltpu.HBM)] * 3,
        scratch_shapes=[dma((3,))],
    )(*results)


def solution(mesh):
    nz, nx = mesh.shape["dp"] // 4, mesh.shape["mp"] // 2
    return jax.shard_map(
        functools.partial(on_device, nz, nx),
        mesh=mesh,
        in_specs=(
            P("dp", "mp"),
            P("dp", "mp"),
            P("mp", None),
            P(("mp", "dp"), None),
            P(("mp", "dp"), None),
            P(("mp", "dp"), None),
        ),
        out_specs=(P(("mp", "dp"), None), P(("mp", "dp"), None), P(("mp", "dp"), None)),
        check_vma=False,
    )
```

```python
import functools

import jax
import jax.numpy as jnp
from jax import lax
from jax.experimental import pallas as pl
from jax.experimental.pallas import tpu as pltpu
from jax.sharding import PartitionSpec as P

beta_one = 0.9
beta_two = 0.99
corr_one = 1.0 - 0.9**10
corr_two = 1.0 - 0.99**10
adam_eps = 1e-08
step_size = 1.0

HUBS = (6, -6, 3, -3, 0)
LEAVES = {6: (8, 7, 5, 6), -6: (-7, -5, -6), 3: (4, 2, 3), -3: (-4, -2, -3), 0: (1, -1, 0)}

MESH = pl.DeviceIdType.MESH
F32 = jnp.float32
BF16 = jnp.bfloat16


def kernel(
    nz, nx, pad,
    acts_hbm, grads_hbm, basis_hbm, weights_hbm, first_hbm, second_hbm,
    weights_out, first_out, second_out,
    acts, grads, basis, weights, first, second,
    part, part_in, proj, turned,
    halves, sibling_in, leaf, hub_in, column, fin_out, fin_in, dirs, blocks, delta,
    load_sem, rs_send, rs_recv, ag_send, ag_recv, core_send, core_recv,
    hub_send, hub_recv, fin_send, fin_recv,
    dir_send, dir_recv, blk_send, blk_recv, relay_sem,
):
    dp, mp = lax.axis_index("dp"), lax.axis_index("mp")
    z, y_hi, core = dp // 4, (dp // 2) % 2, dp % 2
    x, y_lo = mp // 2, mp % 2
    tokens, width = acts.shape
    hidden = turned.shape[0]
    rank = basis.shape[1]
    rows = first.shape[0]
    span = hidden // nz
    piece = tokens // (2 * nx)

    def dp_of(z_at, y_at, core_at):
        return (z_at % nz) * 4 + y_at * 2 + core_at

    def mp_of(r, dy):
        return ((x + r + nx) % nx) * 2 + (y_lo + dy) % 2

    loads = [
        pltpu.make_async_copy(src, dst, load_sem.at[i])
        for i, (src, dst) in enumerate(
            (
                (basis_hbm, basis),
                (acts_hbm, acts),
                (grads_hbm, grads),
                (weights_hbm, weights),
                (first_hbm, first),
                (second_hbm, second),
            )
        )
    ]
    for load in loads[:2]:
        load.start()

    relations = [(r, dy) for r in range(nx) for dy in range(2)]
    peers = [({"mp": mp_of(r, dy)}) for r, dy in relations[1:]]
    peers += [
        {"dp": dp_of(z, y_hi, 1 - core)},
        {"dp": dp_of(z, 1 - y_hi, core)},
        {"dp": dp_of(z + 1, y_hi, core)},
        {"dp": dp_of(z + nz - 1, y_hi, core)},
    ]
    barrier = pltpu.get_barrier_semaphore()
    for peer in peers:
        pl.semaphore_signal(barrier, inc=1, device_id=peer, device_id_type=MESH)

    def tell(n):
        for i, dz in enumerate((n, -n)):
            pl.semaphore_signal(
                relay_sem.at[n - 1, i], inc=1,
                device_id={"dp": dp_of(z + dz + nz, y_hi, core)}, device_id_type=MESH,
            )

    def hear(n):
        for i in range(2):
            pl.semaphore_wait(relay_sem.at[n - 1, i], 1)

    def send(src, dst, send_sem, recv_sem, device):
        copy = pltpu.make_async_remote_copy(
            src_ref=src, dst_ref=dst, send_sem=send_sem, recv_sem=recv_sem,
            device_id=device, device_id_type=MESH,
        )
        copy.start()
        return copy

    loads[0].wait()
    loads[1].wait()
    for load in loads[2:]:
        load.start()

    half = rank // 2

    def piece_of(index):
        return pl.ds(pl.multiple_of(index * piece, piece), piece)

    order = [nx // 2] * (nx > 1) + [r for r in range(1, nx) if r != nx // 2] + [0]
    rs = {}
    for s in range(2):
        value = jnp.dot(
            acts[...], basis[:, s * half : (s + 1) * half], preferred_element_type=F32
        )
        part[s] = value.astype(BF16)
        if s == 0:
            pl.semaphore_wait(barrier, len(peers))
            tell(1)
        for r in order:
            for dy in (1, 0):
                q = 2 * r + dy
                if q:
                    rs[s, q] = send(
                        part.at[s, piece_of(mp_of(r, dy)), :], part_in.at[s, q],
                        rs_send.at[s, q], rs_recv.at[s, q], {"mp": mp_of(r, dy)},
                    )

    loads[2].wait()
    for b in range(hidden // 128):
        turned[pl.ds(b * 128, 128), :] = grads[:, pl.ds(b * 128, 128)].T
    hear(1)
    tell(2)

    ag = {}
    for s in range(2):
        total = part[s, piece_of(mp), :].astype(F32)
        for q in range(1, 2 * nx):
            rs[s, q].wait()
            total = total + part_in[s, q].astype(F32)
        proj[s, piece_of(mp), :] = total.astype(BF16)
        for r in order:
            for dy in (1, 0):
                q = 2 * r + dy
                if q:
                    ag[s, q] = send(
                        proj.at[s, piece_of(mp), :], proj.at[s, piece_of(mp), :],
                        ag_send.at[s, q], ag_recv.at[s, q], {"mp": mp_of(r, dy)},
                    )
    hear(2)
    tell(3)

    schedule = [(h, o) for h in HUBS for o in LEAVES[h]]
    block = rank // 4
    siblings, to_hub = {}, {}

    group = 4

    def multiply(s):
        for b in range(nz // group):
            value = jnp.dot(
                turned[pl.ds(b * group * span, group * span), :], proj[s],
                preferred_element_type=F32,
            ).reshape(group, 2, span // 2, half)
            for c in range(2):
                halves[s, c, pl.ds(b * group, group)] = value[
                    :, :, :, c * block : (c + 1) * block
                ].astype(BF16)
        for n, (h, o) in enumerate(schedule):
            at = (z - o + nz) % nz
            siblings[s, n] = send(
                halves.at[s, 1 - core, at], sibling_in.at[s, n],
                core_send.at[s, n], core_recv.at[s, n], {"dp": dp_of(z, y_hi, 1 - core)},
            )

    def slot(e, dy):
        return (e + 1) * 2 + dy

    def scatter(s, h):
        i = HUBS.index(h)
        members = [n for n in range(nz) if schedule[n][0] == h]
        for n in members:
            siblings[s, n].wait()
        for n in members:
            at = (z - schedule[n][1] + nz) % nz
            value = halves[s, core, at].astype(F32) + sibling_in[s, n].astype(F32)
            leaf[s, n] = value.astype(BF16)
        for n in members:
            e = schedule[n][1] - h
            for dy in (1, 0):
                if e or dy:
                    y_at = (y_hi + dy) % 2
                    to_hub[s, h, e, dy] = send(
                        leaf.at[s, n, y_at], hub_in.at[s, i, slot(e, dy)],
                        hub_send.at[s, i, slot(e, dy)], hub_recv.at[s, i, slot(e, dy)],
                        {"dp": dp_of(z - e + nz, y_at, core)},
                    )

    for s in range(2):
        for q in range(1, 2 * nx):
            ag[s, q].wait()
        multiply(s)
        for h in HUBS:
            scatter(s, h)
    hear(3)

    for load in loads[3:]:
        load.wait()
    column[:, pl.ds(span // 2, 8), :] = jnp.zeros((2, 8, block), F32)
    fin = {}
    for i, h in enumerate(HUBS):
        own = schedule.index((h, h))
        for s in range(2):
            value = leaf[s, own, y_hi].astype(F32)
            for e in [o - h for o in LEAVES[h]]:
                for dy in (0, 1):
                    if e or dy:
                        to_hub[s, h, e, dy].wait()
                        value = value + hub_in[s, i, slot(e, dy)].astype(F32)
            column[s, pl.ds(0, span // 2), :] = value
            for c in range(2):
                cut = column[s, pl.ds(c * rows, pad), :]
                fin_out[i, c, pl.ds(s * pad, pad), :] = cut.astype(BF16)
        for dc in (1, 0):
            core_at = (core + dc) % 2
            if h or dc:
                fin[i, dc] = send(
                    fin_out.at[i, core_at], fin_in.at[i, dc],
                    fin_send.at[i, dc], fin_recv.at[i, dc],
                    {"dp": dp_of(z - h + nz, y_hi, core_at)},
                )

    for dc in range(2):
        for i, h in enumerate(HUBS):
            if h or dc:
                fin[i, dc].wait()
        for k in range(2):
            at = pl.ds(k * pad, pad)
            low_grad = (fin_in if dc else fin_out)[len(HUBS) - 1, 1 if dc else core, at, :].astype(F32)
            for i in range(len(HUBS) - 1):
                low_grad = low_grad + fin_in[i, dc, at, :].astype(F32)
            low_grad = low_grad[:rows]
            cut = pl.ds(pl.multiple_of((2 * k + (core + dc) % 2) * block, block), block)
            moment_new = beta_one * first[:, cut] + (1.0 - beta_one) * low_grad
            second_new = beta_two * second[:, cut] + (1.0 - beta_two) * low_grad * low_grad
            direction = moment_new / corr_one / (jnp.sqrt(second_new / corr_two) + adam_eps)
            first_out[:, cut] = moment_new
            second_out[:, cut] = second_new
            padded = jnp.concatenate([direction, jnp.zeros((pad - rows, block), F32)], axis=0)
            dirs[0, :, cut] = padded.astype(BF16)

    gathered, returned = {}, {}
    for r in order:
        for dy in (1, 0):
            q = 2 * r + dy
            if q:
                gathered[q] = send(
                    dirs.at[0], dirs.at[q], dir_send.at[q], dir_recv.at[q], {"mp": mp_of(r, dy)},
                )
    for r in list(order[::-1]):
        for dy in range(2):
            if 2 * r + dy:
                gathered[2 * r + dy].wait()
        stacked = dirs[pl.ds(2 * r, 2)].reshape(2 * pad, rank)
        product = lax.dot_general(
            stacked, basis[...], (((1,), (1,)), ((), ())), preferred_element_type=F32
        ).astype(BF16)
        for dy in range(2):
            q = 2 * r + dy
            blocks[q] = product[dy * pad : (dy + 1) * pad]
            if q:
                returned[q] = send(
                    blocks.at[q], delta.at[q], blk_send.at[q], blk_recv.at[q], {"mp": mp_of(-r, dy)},
                )
    for r in list(order[::-1]):
        for dy in range(2):
            q = 2 * r + dy
            if q:
                returned[q].wait()
            at = pl.ds(pl.multiple_of(mp_of(r, dy) * width, width), width)
            change = (delta if q else blocks)[q].astype(F32)[:rows]
            weights_out[:, at] = (weights[:, at].astype(F32) - step_size * change).astype(BF16)


def on_device(nz, nx, acts, out_grads, basis, weights, first_moment, second_moment):
    tokens, width = acts.shape
    hidden = out_grads.shape[1]
    rank = basis.shape[1]
    rows, full = weights.shape
    pad = -(-rows // 16) * 16
    span = hidden // nz
    peers = 2 * nx
    piece = tokens // peers
    hubs = len(HUBS)
    arrays = (acts, out_grads, basis, weights, first_moment, second_moment)
    held = [pltpu.with_memory_space_constraint(array, pltpu.HBM) for array in arrays]
    dma = pltpu.SemaphoreType.DMA
    vmem = pltpu.VMEM
    return pl.pallas_call(
        functools.partial(kernel, nz, nx, pad),
        out_shape=(
            jax.ShapeDtypeStruct(weights.shape, BF16),
            jax.ShapeDtypeStruct(first_moment.shape, F32),
            jax.ShapeDtypeStruct(second_moment.shape, F32),
        ),
        in_specs=[pl.BlockSpec(memory_space=pltpu.HBM)] * 6,
        out_specs=[pl.BlockSpec(memory_space=pltpu.VMEM)] * 3,
        scratch_shapes=[
            vmem(acts.shape, BF16),
            vmem(out_grads.shape, BF16),
            vmem(basis.shape, BF16),
            vmem(weights.shape, BF16),
            vmem(first_moment.shape, F32),
            vmem(second_moment.shape, F32),
            vmem((2, tokens, rank // 2), BF16),
            vmem((2, peers, piece, rank // 2), BF16),
            vmem((2, tokens, rank // 2), BF16),
            vmem((hidden, tokens), BF16),
            vmem((2, 2, nz, 2, span // 2, rank // 4), BF16),
            vmem((2, nz, 2, span // 2, rank // 4), BF16),
            vmem((2, nz, 2, span // 2, rank // 4), BF16),
            vmem((2, hubs, 8, span // 2, rank // 4), BF16),
            vmem((2, span // 2 + 8, rank // 4), F32),
            vmem((hubs, 2, 2 * pad, rank // 4), BF16),
            vmem((hubs, 2, 2 * pad, rank // 4), BF16),
            vmem((peers, pad, rank), BF16),
            vmem((peers, pad, width), BF16),
            vmem((peers, pad, width), BF16),
            dma((6,)),
            dma((2, peers)), dma((2, peers)), dma((2, peers)), dma((2, peers)),
            dma((2, nz)), dma((2, nz)),
            dma((2, hubs, 8)), dma((2, hubs, 8)), dma((hubs, 2)), dma((hubs, 2)),
            dma((peers,)), dma((peers,)), dma((peers,)), dma((peers,)),
            pltpu.SemaphoreType.REGULAR((3, 2)),
        ],
        compiler_params=pltpu.CompilerParams(
            collective_id=0, has_side_effects=True, vmem_limit_bytes=32 * 1024 * 1024
        ),
    )(*held)


def solution(mesh):
    nz, nx = mesh.shape["dp"] // 4, mesh.shape["mp"] // 2
    return jax.shard_map(
        functools.partial(on_device, nz, nx),
        mesh=mesh,
        in_specs=(
            P("dp", "mp"),
            P("dp", "mp"),
            P("mp", None),
            P(("mp", "dp"), None),
            P(("mp", "dp"), None),
            P(("mp", "dp"), None),
        ),
        out_specs=(P(("mp", "dp"), None), P(("mp", "dp"), None), P(("mp", "dp"), None)),
        check_vma=False,
    )
```

```python
import functools

import jax
import jax.numpy as jnp
from jax import lax
from jax.experimental import pallas as pl
from jax.experimental.pallas import tpu as pltpu
from jax.sharding import PartitionSpec as P

beta_one = 0.9
beta_two = 0.99
corr_one = 1.0 - 0.9**10
corr_two = 1.0 - 0.99**10
adam_eps = 1e-08
step_size = 1.0

HUBS = (6, -6, 3, -3, 0)
HELPERS = ((0, "row"), (1, "row"), (-1, "row"), (0, "inner"), (0, "outer"), (1, "inner"), (-1, "outer"))
LEAVES = {6: (8, 7, 5, 6), -6: (-7, -5, -6), 3: (4, 2, 3), -3: (-4, -2, -3), 0: (1, -1, 0)}

MESH = pl.DeviceIdType.MESH
F32 = jnp.float32
BF16 = jnp.bfloat16


def moments(first, second, low_grad):
    moment_new = beta_one * first + (1.0 - beta_one) * low_grad
    second_new = beta_two * second + (1.0 - beta_two) * low_grad * low_grad
    return moment_new, second_new


def kernel(
    nz, nx, pad,
    acts_hbm, grads_hbm, basis_hbm, weights_hbm, first_hbm, second_hbm,
    weights_out, grad_out,
    acts, grads, basis, weights, first, second,
    part, part_in, proj, turned,
    halves, sibling_in, leaf, hub_in, column, fin_out, fin_in, dirs, blocks, delta,
    load_sem, rs_send, rs_recv, ag_send, ag_recv, core_send, core_recv,
    hub_send, hub_recv, fin_send, fin_recv,
    dir_send, dir_recv, blk_send, blk_recv, relay_sem, far_basis, far_send, far_recv,
):
    dp, mp = lax.axis_index("dp"), lax.axis_index("mp")
    z, y_hi, core = dp // 4, (dp // 2) % 2, dp % 2
    x, y_lo = mp // 2, mp % 2
    tokens, width = acts.shape
    hidden = turned.shape[0]
    rank = basis.shape[1]
    rows = first.shape[0]
    span = hidden // nz
    piece = tokens // (2 * nx)

    def dp_of(z_at, y_at, core_at):
        return (z_at % nz) * 4 + y_at * 2 + core_at

    def mp_of(r, dy):
        return ((x + r + nx) % nx) * 2 + (y_lo + dy) % 2

    def device_of(r, via):
        y_at = 1 - y_hi if via == "outer" else y_hi
        return {"dp": dp_of(z, y_at, core), "mp": mp_of(r, 0 if via == "row" else 1)}

    loads = [
        pltpu.make_async_copy(src, dst, load_sem.at[i])
        for i, (src, dst) in enumerate(
            (
                (basis_hbm, basis),
                (acts_hbm, acts),
                (grads_hbm, grads),
                (weights_hbm, weights),
                (first_hbm, first),
                (second_hbm, second),
            )
        )
    ]
    for load in loads[:2]:
        load.start()

    relations = [(r, dy) for r in range(nx) for dy in range(2)]
    peers = [({"mp": mp_of(r, dy)}) for r, dy in relations[1:]]
    peers += [
        {"dp": dp_of(z, y_hi, 1 - core)},
        {"dp": dp_of(z, 1 - y_hi, core)},
        {"dp": dp_of(z + 1, y_hi, core)},
        {"dp": dp_of(z + nz - 1, y_hi, core)},
    ]
    peers += [device_of(r, "outer") for r in (-1, 0, 1)]
    barrier = pltpu.get_barrier_semaphore()
    for peer in peers:
        pl.semaphore_signal(barrier, inc=1, device_id=peer, device_id_type=MESH)

    def tell(n):
        for i, dz in enumerate((n, -n)):
            pl.semaphore_signal(
                relay_sem.at[n - 1, i], inc=1,
                device_id={"dp": dp_of(z + dz + nz, y_hi, core)}, device_id_type=MESH,
            )

    def hear(n):
        for i in range(2):
            pl.semaphore_wait(relay_sem.at[n - 1, i], 1)

    def send(src, dst, send_sem, recv_sem, device):
        copy = pltpu.make_async_remote_copy(
            src_ref=src, dst_ref=dst, send_sem=send_sem, recv_sem=recv_sem,
            device_id=device, device_id_type=MESH,
        )
        copy.start()
        return copy

    loads[0].wait()
    loads[1].wait()
    for load in loads[2:]:
        load.start()

    half = rank // 2

    def piece_of(index):
        return pl.ds(pl.multiple_of(index * piece, piece), piece)

    order = [nx // 2] * (nx > 1) + [r for r in range(1, nx) if r != nx // 2] + [0]
    rs = {}
    for s in range(2):
        value = jnp.dot(
            acts[...], basis[:, s * half : (s + 1) * half], preferred_element_type=F32
        )
        part[s] = value.astype(BF16)
        if s == 0:
            pl.semaphore_wait(barrier, len(peers))
            tell(1)
        for r in order:
            for dy in (1, 0):
                q = 2 * r + dy
                if q:
                    rs[s, q] = send(
                        part.at[s, piece_of(mp_of(r, dy)), :], part_in.at[s, q],
                        rs_send.at[s, q], rs_recv.at[s, q], {"mp": mp_of(r, dy)},
                    )

    loads[2].wait()
    for b in range(hidden // 128):
        turned[pl.ds(b * 128, 128), :] = grads[:, pl.ds(b * 128, 128)].T
    hear(1)
    tell(2)

    ag = {}
    for s in range(2):
        total = part[s, piece_of(mp), :].astype(F32)
        for q in range(1, 2 * nx):
            rs[s, q].wait()
            total = total + part_in[s, q].astype(F32)
        proj[s, piece_of(mp), :] = total.astype(BF16)
        for r in order:
            for dy in (1, 0):
                q = 2 * r + dy
                if q:
                    ag[s, q] = send(
                        proj.at[s, piece_of(mp), :], proj.at[s, piece_of(mp), :],
                        ag_send.at[s, q], ag_recv.at[s, q], {"mp": mp_of(r, dy)},
                    )
    hear(2)
    tell(3)

    schedule = [(h, o) for h in HUBS for o in LEAVES[h]]
    block = rank // 4
    siblings, to_hub = {}, {}

    group = 4

    def multiply(s):
        for b in range(nz // group):
            value = jnp.dot(
                turned[pl.ds(b * group * span, group * span), :], proj[s],
                preferred_element_type=F32,
            ).reshape(group, 2, span // 2, half)
            for c in range(2):
                halves[s, c, pl.ds(b * group, group)] = value[
                    :, :, :, c * block : (c + 1) * block
                ].astype(BF16)
        for n, (h, o) in enumerate(schedule):
            at = (z - o + nz) % nz
            siblings[s, n] = send(
                halves.at[s, 1 - core, at], sibling_in.at[s, n],
                core_send.at[s, n], core_recv.at[s, n], {"dp": dp_of(z, y_hi, 1 - core)},
            )

    def slot(e, dy):
        return (e + 1) * 2 + dy

    def scatter(s, h):
        i = HUBS.index(h)
        members = [n for n in range(nz) if schedule[n][0] == h]
        for n in members:
            siblings[s, n].wait()
        for n in members:
            at = (z - schedule[n][1] + nz) % nz
            value = halves[s, core, at].astype(F32) + sibling_in[s, n].astype(F32)
            leaf[s, n] = value.astype(BF16)
        for n in members:
            e = schedule[n][1] - h
            for dy in (1, 0):
                if e or dy:
                    y_at = (y_hi + dy) % 2
                    to_hub[s, h, e, dy] = send(
                        leaf.at[s, n, y_at], hub_in.at[s, i, slot(e, dy)],
                        hub_send.at[s, i, slot(e, dy)], hub_recv.at[s, i, slot(e, dy)],
                        {"dp": dp_of(z - e + nz, y_at, core)},
                    )

    for s in range(2):
        for q in range(1, 2 * nx):
            ag[s, q].wait()
        if s == 1:
            mine = pl.ds(pl.multiple_of(core * (width // 2), width // 2), width // 2)
            far = send(
                basis.at[mine, :], far_basis.at[mine, :], far_send.at[0], far_recv.at[0],
                device_of(2, "row"),
            )
        multiply(s)
        for h in HUBS:
            scatter(s, h)
    hear(3)

    for load in loads[3:]:
        load.wait()
    column[:, pl.ds(span // 2, 8), :] = jnp.zeros((2, 8, block), F32)
    fin = {}
    for i, h in enumerate(HUBS):
        own = schedule.index((h, h))
        for s in range(2):
            value = leaf[s, own, y_hi].astype(F32)
            for e in [o - h for o in LEAVES[h]]:
                for dy in (0, 1):
                    if e or dy:
                        to_hub[s, h, e, dy].wait()
                        value = value + hub_in[s, i, slot(e, dy)].astype(F32)
            column[s, pl.ds(0, span // 2), :] = value
            for c in range(2):
                cut = column[s, pl.ds(c * rows, pad), :]
                fin_out[i, c, pl.ds(s * pad, pad), :] = cut.astype(BF16)
        for dc in (1, 0):
            core_at = (core + dc) % 2
            if h or dc:
                fin[i, dc] = send(
                    fin_out.at[i, core_at], fin_in.at[i, dc],
                    fin_send.at[i, dc], fin_recv.at[i, dc],
                    {"dp": dp_of(z - h + nz, y_hi, core_at)},
                )

    far.wait()
    swap = send(
        far_basis.at[mine, :], far_basis.at[mine, :], far_send.at[1], far_recv.at[1],
        {"dp": dp_of(z, y_hi, 1 - core)},
    )
    for dc in range(2):
        for i, h in enumerate(HUBS):
            if h or dc:
                fin[i, dc].wait()
        for k in range(2):
            at = pl.ds(k * pad, pad)
            low_grad = (fin_in if dc else fin_out)[len(HUBS) - 1, 1 if dc else core, at, :].astype(F32)
            for i in range(len(HUBS) - 1):
                low_grad = low_grad + fin_in[i, dc, at, :].astype(F32)
            low_grad = low_grad[:rows]
            cut = pl.ds(pl.multiple_of((2 * k + (core + dc) % 2) * block, block), block)
            moment_new, second_new = moments(first[:, cut], second[:, cut], low_grad)
            direction = moment_new / corr_one / (jnp.sqrt(second_new / corr_two) + adam_eps)
            grad_out[:, cut] = low_grad
            padded = jnp.concatenate([direction, jnp.zeros((pad - rows, block), F32)], axis=0)
            dirs[0, :, cut] = padded.astype(BF16)

    gathered, returned = {}, {}
    for k in (5, 6, 4, 3, 1, 2):
        gathered[k] = send(
            dirs.at[0], dirs.at[k], dir_send.at[k], dir_recv.at[k], device_of(*HELPERS[k]),
        )

    def update(slots, shard):
        stacked = jnp.concatenate([dirs[k] for k in slots], axis=0)
        product = lax.dot_general(
            stacked, shard[...], (((1,), (1,)), ((), ())), preferred_element_type=F32
        ).astype(BF16)
        return [product[i * pad : (i + 1) * pad] for i in range(len(slots))]

    def give_back(k, value):
        r, via = HELPERS[k]
        blocks[k] = value
        returned[k] = send(
            blocks.at[k], delta.at[k], blk_send.at[k], blk_recv.at[k], device_of(-r, via),
        )

    def apply(r, via, change):
        at = pl.ds(pl.multiple_of(mp_of(r, 0 if via == "row" else 1) * width, width), width)
        change = change.astype(F32)[:rows]
        weights_out[:, at] = (weights[:, at].astype(F32) - step_size * change).astype(BF16)

    near = (5, 6, 3, 1, 2)
    for k in near:
        gathered[k].wait()
    for k, value in zip(near, update(near, basis)):
        give_back(k, value)
    swap.wait()
    gathered[4].wait()
    value, own = update((4, 0), far_basis)
    give_back(4, value)
    apply(2, "row", own)
    apply(0, "row", update((0,), basis)[0])
    for k in (3, 1, 2, 4, 5, 6):
        returned[k].wait()
        r, via = HELPERS[k]
        apply(r + 2 if k == 4 else r, via, delta[k])


def on_device(nz, nx, acts, out_grads, basis, weights, first_moment, second_moment):
    tokens, width = acts.shape
    hidden = out_grads.shape[1]
    rank = basis.shape[1]
    rows, full = weights.shape
    pad = -(-rows // 16) * 16
    span = hidden // nz
    peers = 2 * nx
    piece = tokens // peers
    hubs = len(HUBS)
    arrays = (acts, out_grads, basis, weights, first_moment, second_moment)
    held = [pltpu.with_memory_space_constraint(array, pltpu.HBM) for array in arrays]
    dma = pltpu.SemaphoreType.DMA
    vmem = pltpu.VMEM
    new_weights, low_grad = pl.pallas_call(
        functools.partial(kernel, nz, nx, pad),
        out_shape=(
            jax.ShapeDtypeStruct(weights.shape, BF16),
            jax.ShapeDtypeStruct(first_moment.shape, F32),
        ),
        in_specs=[pl.BlockSpec(memory_space=pltpu.HBM)] * 6,
        out_specs=[pl.BlockSpec(memory_space=pltpu.VMEM)] * 2,
        scratch_shapes=[
            vmem(acts.shape, BF16),
            vmem(out_grads.shape, BF16),
            vmem(basis.shape, BF16),
            vmem(weights.shape, BF16),
            vmem(first_moment.shape, F32),
            vmem(second_moment.shape, F32),
            vmem((2, tokens, rank // 2), BF16),
            vmem((2, peers, piece, rank // 2), BF16),
            vmem((2, tokens, rank // 2), BF16),
            vmem((hidden, tokens), BF16),
            vmem((2, 2, nz, 2, span // 2, rank // 4), BF16),
            vmem((2, nz, 2, span // 2, rank // 4), BF16),
            vmem((2, nz, 2, span // 2, rank // 4), BF16),
            vmem((2, hubs, 8, span // 2, rank // 4), BF16),
            vmem((2, span // 2 + 8, rank // 4), F32),
            vmem((hubs, 2, 2 * pad, rank // 4), BF16),
            vmem((hubs, 2, 2 * pad, rank // 4), BF16),
            vmem((peers, pad, rank), BF16),
            vmem((peers, pad, width), BF16),
            vmem((peers, pad, width), BF16),
            dma((6,)),
            dma((2, peers)), dma((2, peers)), dma((2, peers)), dma((2, peers)),
            dma((2, nz)), dma((2, nz)),
            dma((2, hubs, 8)), dma((2, hubs, 8)), dma((hubs, 2)), dma((hubs, 2)),
            dma((peers,)), dma((peers,)), dma((peers,)), dma((peers,)),
            pltpu.SemaphoreType.REGULAR((3, 2)),
            vmem(basis.shape, BF16),
            dma((2,)), dma((2,)),
        ],
        compiler_params=pltpu.CompilerParams(
            collective_id=0, has_side_effects=True, vmem_limit_bytes=32 * 1024 * 1024
        ),
    )(*held)
    moment_new, second_new = moments(first_moment, second_moment, low_grad)
    return new_weights, moment_new, second_new


def solution(mesh):
    nz, nx = mesh.shape["dp"] // 4, mesh.shape["mp"] // 2
    return jax.shard_map(
        functools.partial(on_device, nz, nx),
        mesh=mesh,
        in_specs=(
            P("dp", "mp"),
            P("dp", "mp"),
            P("mp", None),
            P(("mp", "dp"), None),
            P(("mp", "dp"), None),
            P(("mp", "dp"), None),
        ),
        out_specs=(P(("mp", "dp"), None), P(("mp", "dp"), None), P(("mp", "dp"), None)),
        check_vma=False,
    )
```

```python
import functools

import jax
import jax.numpy as jnp
from jax import lax
from jax.experimental import pallas as pl
from jax.experimental.pallas import tpu as pltpu
from jax.sharding import PartitionSpec as P

beta_one = 0.9
beta_two = 0.99
corr_one = 1.0 - 0.9**10
corr_two = 1.0 - 0.99**10
adam_eps = 1e-08
step_size = 1.0

HUBS = (6, -6, 0, 3, -3)
HELPERS = ((0, "row"), (1, "row"), (-1, "row"), (0, "inner"), (0, "outer"), (1, "inner"), (-1, "outer"))
LEAVES = {6: (8, 7, 5, 6), -6: (-7, -5, -6), 3: (4, 2, 3), -3: (-4, -2, -3), 0: (1, -1, 0)}

MESH = pl.DeviceIdType.MESH
F32 = jnp.float32
BF16 = jnp.bfloat16


def moments(first, second, low_grad):
    moment_new = beta_one * first + (1.0 - beta_one) * low_grad
    second_new = beta_two * second + (1.0 - beta_two) * low_grad * low_grad
    return moment_new, second_new


def kernel(
    nz, nx, pad,
    acts_hbm, grads_hbm, basis_hbm, weights_hbm, first_hbm, second_hbm,
    weights_out, grad_out,
    acts, grads, basis, weights, first, second,
    part, part_in, proj, turned,
    halves, sibling_in, leaf, hub_in, column, fin_out, fin_in, dirs, blocks, delta,
    load_sem, rs_send, rs_recv, ag_send, ag_recv, core_send, core_recv,
    hub_send, hub_recv, fin_send, fin_recv,
    dir_send, dir_recv, blk_send, blk_recv, relay_sem, far_basis, far_send, far_recv,
):
    dp, mp = lax.axis_index("dp"), lax.axis_index("mp")
    z, y_hi, core = dp // 4, (dp // 2) % 2, dp % 2
    x, y_lo = mp // 2, mp % 2
    tokens, width = acts.shape
    hidden = turned.shape[0]
    rank = basis.shape[1]
    rows = first.shape[0]
    span = hidden // nz
    piece = tokens // (2 * nx)

    def dp_of(z_at, y_at, core_at):
        return (z_at % nz) * 4 + y_at * 2 + core_at

    def mp_of(r, dy):
        return ((x + r + nx) % nx) * 2 + (y_lo + dy) % 2

    def device_of(r, via):
        y_at = 1 - y_hi if via == "outer" else y_hi
        return {"dp": dp_of(z, y_at, core), "mp": mp_of(r, 0 if via == "row" else 1)}

    loads = [
        pltpu.make_async_copy(src, dst, load_sem.at[i])
        for i, (src, dst) in enumerate(
            (
                (basis_hbm, basis),
                (acts_hbm, acts),
                (grads_hbm, grads),
                (weights_hbm, weights),
                (first_hbm, first),
                (second_hbm, second),
            )
        )
    ]
    for load in loads[:2]:
        load.start()

    relations = [(r, dy) for r in range(nx) for dy in range(2)]
    peers = [({"mp": mp_of(r, dy)}) for r, dy in relations[1:]]
    peers += [
        {"dp": dp_of(z, y_hi, 1 - core)},
        {"dp": dp_of(z, 1 - y_hi, core)},
        {"dp": dp_of(z + 1, y_hi, core)},
        {"dp": dp_of(z + nz - 1, y_hi, core)},
    ]
    peers += [device_of(r, "outer") for r in (-1, 0, 1)]
    peers += [{"dp": dp_of(z, 1 - y_hi, 1 - core)}]
    barrier = pltpu.get_barrier_semaphore()
    for peer in peers:
        pl.semaphore_signal(barrier, inc=1, device_id=peer, device_id_type=MESH)

    def tell(n):
        for i, dz in enumerate((n, -n)):
            pl.semaphore_signal(
                relay_sem.at[n - 1, i], inc=1,
                device_id={"dp": dp_of(z + dz + nz, y_hi, core)}, device_id_type=MESH,
            )

    def hear(n):
        for i in range(2):
            pl.semaphore_wait(relay_sem.at[n - 1, i], 1)

    def send(src, dst, send_sem, recv_sem, device):
        copy = pltpu.make_async_remote_copy(
            src_ref=src, dst_ref=dst, send_sem=send_sem, recv_sem=recv_sem,
            device_id=device, device_id_type=MESH,
        )
        copy.start()
        return copy

    loads[0].wait()
    loads[1].wait()
    for load in loads[2:]:
        load.start()

    half = rank // 2

    def piece_of(index):
        return pl.ds(pl.multiple_of(index * piece, piece), piece)

    order = [nx // 2] * (nx > 1) + [r for r in range(1, nx) if r != nx // 2] + [0]
    rs = {}
    for s in range(2):
        value = jnp.dot(
            acts[...], basis[:, s * half : (s + 1) * half], preferred_element_type=F32
        )
        part[s] = value.astype(BF16)
        if s == 0:
            pl.semaphore_wait(barrier, len(peers))
            tell(1)
        for r in order:
            for dy in (1, 0):
                q = 2 * r + dy
                if q:
                    rs[s, q] = send(
                        part.at[s, piece_of(mp_of(r, dy)), :], part_in.at[s, q],
                        rs_send.at[s, q], rs_recv.at[s, q], {"mp": mp_of(r, dy)},
                    )

    loads[2].wait()
    for b in range(hidden // 128):
        turned[pl.ds(b * 128, 128), :] = grads[:, pl.ds(b * 128, 128)].T
    hear(1)
    tell(2)

    ag = {}
    for s in range(2):
        total = part[s, piece_of(mp), :].astype(F32)
        for q in range(1, 2 * nx):
            rs[s, q].wait()
            total = total + part_in[s, q].astype(F32)
        proj[s, piece_of(mp), :] = total.astype(BF16)
        for r in order:
            for dy in (1, 0):
                q = 2 * r + dy
                if q:
                    ag[s, q] = send(
                        proj.at[s, piece_of(mp), :], proj.at[s, piece_of(mp), :],
                        ag_send.at[s, q], ag_recv.at[s, q], {"mp": mp_of(r, dy)},
                    )
    hear(2)
    tell(3)

    schedule = [(h, o) for h in HUBS for o in LEAVES[h]]
    block = rank // 4
    siblings, to_hub = {}, {}

    group = 4

    def multiply(s):
        for b in range(nz // group):
            value = jnp.dot(
                turned[pl.ds(b * group * span, group * span), :], proj[s],
                preferred_element_type=F32,
            ).reshape(group, 2, span // 2, half)
            for c in range(2):
                halves[s, c, pl.ds(b * group, group)] = value[
                    :, :, :, c * block : (c + 1) * block
                ].astype(BF16)
        for n, (h, o) in enumerate(schedule):
            at = (z - o + nz) % nz
            siblings[s, n] = send(
                halves.at[s, 1 - core, at], sibling_in.at[s, n],
                core_send.at[s, n], core_recv.at[s, n], {"dp": dp_of(z, y_hi, 1 - core)},
            )

    def slot(e, dy):
        return (e + 1) * 2 + dy

    def scatter(s, h):
        i = HUBS.index(h)
        members = [n for n in range(nz) if schedule[n][0] == h]
        for n in members:
            siblings[s, n].wait()
        for n in members:
            at = (z - schedule[n][1] + nz) % nz
            value = halves[s, core, at].astype(F32) + sibling_in[s, n].astype(F32)
            leaf[s, n] = value.astype(BF16)
        for n in members:
            e = schedule[n][1] - h
            if h == 0:
                for y in range(2):
                    if e:
                        to_hub[s, 0, e, y] = send(
                            leaf.at[s, n, y], hub_in.at[s, i, slot(e, y)],
                            hub_send.at[s, i, slot(e, y)], hub_recv.at[s, i, slot(e, y)],
                            {"dp": dp_of(z - e + nz, y_hi, core)},
                        )
                continue
            for dy in (1, 0):
                if e or dy:
                    y_at = (y_hi + dy) % 2
                    to_hub[s, h, e, dy] = send(
                        leaf.at[s, n, y_at], hub_in.at[s, i, slot(e, dy)],
                        hub_send.at[s, i, slot(e, dy)], hub_recv.at[s, i, slot(e, dy)],
                        {"dp": dp_of(z - e + nz, y_at, core)},
                    )

    for s in range(2):
        for q in range(1, 2 * nx):
            ag[s, q].wait()
        if s == 1:
            mine = pl.ds(pl.multiple_of(core * (width // 2), width // 2), width // 2)
            far = send(
                basis.at[mine, :], far_basis.at[mine, :], far_send.at[0], far_recv.at[0],
                device_of(2, "row"),
            )
        multiply(s)
        for h in HUBS:
            scatter(s, h)
    hear(3)

    for load in loads[3:]:
        load.wait()
    column[:, pl.ds(span // 2, 8), :] = jnp.zeros((2, 8, block), F32)
    fin = {}
    home = HUBS.index(0)

    def collect(i, h, v, into):
        own = schedule.index((h, h))
        for s in range(2):
            value = leaf[s, own, (y_hi + v) % 2].astype(F32)
            for e in [o - h for o in LEAVES[h]]:
                for dy in (0, 1):
                    if (e or (dy and h)) and not v:
                        to_hub[s, h, e, dy].wait()
            for e in [o - h for o in LEAVES[h]]:
                if h == 0:
                    if e:
                        value = value + hub_in[s, i, slot(e, 0) + (y_hi + v) % 2].astype(F32)
                    continue
                for dy in (0, 1):
                    if e or dy:
                        value = value + hub_in[s, i, slot(e, dy)].astype(F32)
            column[s, pl.ds(0, span // 2), :] = value
            for c in range(2):
                cut = column[s, pl.ds(c * rows, pad), :]
                fin_out[into, c, pl.ds(s * pad, pad), :] = cut.astype(BF16)
        for dc in (1, 0):
            core_at = (core + dc) % 2
            if h or v or dc:
                fin[into, dc] = send(
                    fin_out.at[into, core_at], fin_in.at[into, dc],
                    fin_send.at[into, dc], fin_recv.at[into, dc],
                    {"dp": dp_of(z - h + nz, (y_hi + v) % 2, core_at)},
                )

    for i, h in enumerate(HUBS):
        collect(i, h, 0, i)
        if h == 0:
            collect(i, 0, 1, len(HUBS))

    far.wait()
    swap = send(
        far_basis.at[mine, :], far_basis.at[mine, :], far_send.at[1], far_recv.at[1],
        {"dp": dp_of(z, y_hi, 1 - core)},
    )
    for dc in range(2):
        for i in range(len(HUBS) + 1):
            if i != home or dc:
                fin[i, dc].wait()
        for k in range(2):
            at = pl.ds(k * pad, pad)
            low_grad = (fin_in if dc else fin_out)[home, 1 if dc else core, at, :].astype(F32)
            for i in range(len(HUBS) + 1):
                if i != home:
                    low_grad = low_grad + fin_in[i, dc, at, :].astype(F32)
            low_grad = low_grad[:rows]
            cut = pl.ds(pl.multiple_of((2 * k + (core + dc) % 2) * block, block), block)
            moment_new, second_new = moments(first[:, cut], second[:, cut], low_grad)
            direction = moment_new / corr_one / (jnp.sqrt(second_new / corr_two) + adam_eps)
            grad_out[:, cut] = low_grad
            padded = jnp.concatenate([direction, jnp.zeros((pad - rows, block), F32)], axis=0)
            dirs[0, :, cut] = padded.astype(BF16)

    gathered, returned = {}, {}
    for k in (5, 6, 4, 3, 1, 2):
        gathered[k] = send(
            dirs.at[0], dirs.at[k], dir_send.at[k], dir_recv.at[k], device_of(*HELPERS[k]),
        )

    def update(slots, shard):
        stacked = jnp.concatenate([dirs[k] for k in slots], axis=0)
        product = lax.dot_general(
            stacked, shard[...], (((1,), (1,)), ((), ())), preferred_element_type=F32
        ).astype(BF16)
        return [product[i * pad : (i + 1) * pad] for i in range(len(slots))]

    def give_back(k, value):
        r, via = HELPERS[k]
        blocks[k] = value
        returned[k] = send(
            blocks.at[k], delta.at[k], blk_send.at[k], blk_recv.at[k], device_of(-r, via),
        )

    def apply(r, via, change):
        at = pl.ds(pl.multiple_of(mp_of(r, 0 if via == "row" else 1) * width, width), width)
        change = change.astype(F32)[:rows]
        weights_out[:, at] = (weights[:, at].astype(F32) - step_size * change).astype(BF16)

    near = (5, 6, 3, 1, 2)
    for k in near:
        gathered[k].wait()
    for k, value in zip(near, update(near, basis)):
        give_back(k, value)
    swap.wait()
    gathered[4].wait()
    value, own = update((4, 0), far_basis)
    give_back(4, value)
    apply(2, "row", own)
    apply(0, "row", update((0,), basis)[0])
    for k in (3, 1, 2, 4, 5, 6):
        returned[k].wait()
        r, via = HELPERS[k]
        apply(r + 2 if k == 4 else r, via, delta[k])


def on_device(nz, nx, acts, out_grads, basis, weights, first_moment, second_moment):
    tokens, width = acts.shape
    hidden = out_grads.shape[1]
    rank = basis.shape[1]
    rows, full = weights.shape
    pad = -(-rows // 16) * 16
    span = hidden // nz
    peers = 2 * nx
    piece = tokens // peers
    hubs = len(HUBS)
    arrays = (acts, out_grads, basis, weights, first_moment, second_moment)
    held = [pltpu.with_memory_space_constraint(array, pltpu.HBM) for array in arrays]
    dma = pltpu.SemaphoreType.DMA
    vmem = pltpu.VMEM
    new_weights, low_grad = pl.pallas_call(
        functools.partial(kernel, nz, nx, pad),
        out_shape=(
            jax.ShapeDtypeStruct(weights.shape, BF16),
            jax.ShapeDtypeStruct(first_moment.shape, F32),
        ),
        in_specs=[pl.BlockSpec(memory_space=pltpu.HBM)] * 6,
        out_specs=[pl.BlockSpec(memory_space=pltpu.VMEM)] * 2,
        scratch_shapes=[
            vmem(acts.shape, BF16),
            vmem(out_grads.shape, BF16),
            vmem(basis.shape, BF16),
            vmem(weights.shape, BF16),
            vmem(first_moment.shape, F32),
            vmem(second_moment.shape, F32),
            vmem((2, tokens, rank // 2), BF16),
            vmem((2, peers, piece, rank // 2), BF16),
            vmem((2, tokens, rank // 2), BF16),
            vmem((hidden, tokens), BF16),
            vmem((2, 2, nz, 2, span // 2, rank // 4), BF16),
            vmem((2, nz, 2, span // 2, rank // 4), BF16),
            vmem((2, nz, 2, span // 2, rank // 4), BF16),
            vmem((2, hubs, 8, span // 2, rank // 4), BF16),
            vmem((2, span // 2 + 8, rank // 4), F32),
            vmem((hubs + 1, 2, 2 * pad, rank // 4), BF16),
            vmem((hubs + 1, 2, 2 * pad, rank // 4), BF16),
            vmem((peers, pad, rank), BF16),
            vmem((peers, pad, width), BF16),
            vmem((peers, pad, width), BF16),
            dma((6,)),
            dma((2, peers)), dma((2, peers)), dma((2, peers)), dma((2, peers)),
            dma((2, nz)), dma((2, nz)),
            dma((2, hubs, 8)), dma((2, hubs, 8)), dma((hubs + 1, 2)), dma((hubs + 1, 2)),
            dma((peers,)), dma((peers,)), dma((peers,)), dma((peers,)),
            pltpu.SemaphoreType.REGULAR((3, 2)),
            vmem(basis.shape, BF16),
            dma((2,)), dma((2,)),
        ],
        compiler_params=pltpu.CompilerParams(
            collective_id=0, has_side_effects=True, vmem_limit_bytes=32 * 1024 * 1024
        ),
    )(*held)
    moment_new, second_new = moments(first_moment, second_moment, low_grad)
    return new_weights, moment_new, second_new


def solution(mesh):
    nz, nx = mesh.shape["dp"] // 4, mesh.shape["mp"] // 2
    return jax.shard_map(
        functools.partial(on_device, nz, nx),
        mesh=mesh,
        in_specs=(
            P("dp", "mp"),
            P("dp", "mp"),
            P("mp", None),
            P(("mp", "dp"), None),
            P(("mp", "dp"), None),
            P(("mp", "dp"), None),
        ),
        out_specs=(P(("mp", "dp"), None), P(("mp", "dp"), None), P(("mp", "dp"), None)),
        check_vma=False,
    )
```

```python
import functools

import jax
import jax.numpy as jnp
from jax import lax
from jax.experimental import pallas as pl
from jax.experimental.pallas import tpu as pltpu
from jax.sharding import PartitionSpec as P

beta_one = 0.9
beta_two = 0.99
corr_one = 1.0 - 0.9**10
corr_two = 1.0 - 0.99**10
adam_eps = 1e-08
step_size = 1.0

HUBS = (6, -6, 0, 3, -3)
HELPERS = ((0, "row"), (1, "row"), (-1, "row"), (0, "inner"), (0, "outer"), (1, "inner"), (-1, "outer"))
NEAR = {3: (4, 2, 3), -3: (-4, -2, -3), 0: (1, -1, 0)}
LEAVES = (
    {6: (8, 7, 5, 6), -6: (-7, -5, -6), **NEAR},
    {6: (7, 5, 6), -6: (-8, -7, -5, -6), **NEAR},
)

MESH = pl.DeviceIdType.MESH
F32 = jnp.float32
BF16 = jnp.bfloat16


def moments(first, second, low_grad):
    moment_new = beta_one * first + (1.0 - beta_one) * low_grad
    second_new = beta_two * second + (1.0 - beta_two) * low_grad * low_grad
    return moment_new, second_new


def kernel(
    nz, nx, pad,
    acts_hbm, grads_hbm, basis_hbm, weights_hbm, first_hbm, second_hbm,
    weights_out, grad_out,
    acts, grads, basis, weights, first, second,
    part, part_in, proj, turned,
    halves, sibling_in, leaf, hub_in, column, fin_out, fin_in, dirs, blocks, delta,
    load_sem, rs_send, rs_recv, ag_send, ag_recv, core_send, core_recv,
    hub_send, hub_recv, fin_send, fin_recv,
    dir_send, dir_recv, blk_send, blk_recv, relay_sem, far_basis, far_send, far_recv,
):
    dp, mp = lax.axis_index("dp"), lax.axis_index("mp")
    z, y_hi, core = dp // 4, (dp // 2) % 2, dp % 2
    x, y_lo = mp // 2, mp % 2
    tokens, width = acts.shape
    hidden = turned.shape[0]
    rank = basis.shape[1]
    rows = first.shape[0]
    span = hidden // nz
    piece = tokens // (2 * nx)

    def dp_of(z_at, y_at, core_at):
        return (z_at % nz) * 4 + y_at * 2 + core_at

    def mp_of(r, dy):
        return ((x + r + nx) % nx) * 2 + (y_lo + dy) % 2

    def device_of(r, via):
        y_at = 1 - y_hi if via == "outer" else y_hi
        return {"dp": dp_of(z, y_at, core), "mp": mp_of(r, 0 if via == "row" else 1)}

    loads = [
        pltpu.make_async_copy(src, dst, load_sem.at[i])
        for i, (src, dst) in enumerate(
            (
                (basis_hbm, basis),
                (acts_hbm, acts),
                (grads_hbm, grads),
                (weights_hbm, weights),
                (first_hbm, first),
                (second_hbm, second),
            )
        )
    ]
    for load in loads[:2]:
        load.start()

    relations = [(r, dy) for r in range(nx) for dy in range(2)]
    peers = [({"mp": mp_of(r, dy)}) for r, dy in relations[1:]]
    peers += [
        {"dp": dp_of(z, y_hi, 1 - core)},
        {"dp": dp_of(z, 1 - y_hi, core)},
        {"dp": dp_of(z + 1, y_hi, core)},
        {"dp": dp_of(z + nz - 1, y_hi, core)},
    ]
    peers += [device_of(r, "outer") for r in (-1, 0, 1)]
    peers += [{"dp": dp_of(z, 1 - y_hi, 1 - core)}]
    barrier = pltpu.get_barrier_semaphore()
    for peer in peers:
        pl.semaphore_signal(barrier, inc=1, device_id=peer, device_id_type=MESH)

    def tell(n):
        for i, dz in enumerate((n, -n)):
            pl.semaphore_signal(
                relay_sem.at[n - 1, i], inc=1,
                device_id={"dp": dp_of(z + dz + nz, y_hi, core)}, device_id_type=MESH,
            )

    def hear(n):
        for i in range(2):
            pl.semaphore_wait(relay_sem.at[n - 1, i], 1)

    def send(src, dst, send_sem, recv_sem, device):
        copy = pltpu.make_async_remote_copy(
            src_ref=src, dst_ref=dst, send_sem=send_sem, recv_sem=recv_sem,
            device_id=device, device_id_type=MESH,
        )
        copy.start()
        return copy

    loads[0].wait()
    loads[1].wait()
    for load in loads[2:]:
        load.start()

    half = rank // 2

    def piece_of(index):
        return pl.ds(pl.multiple_of(index * piece, piece), piece)

    order = [nx // 2] * (nx > 1) + [r for r in range(1, nx) if r != nx // 2] + [0]
    rs = {}
    for s in range(2):
        value = jnp.dot(
            acts[...], basis[:, s * half : (s + 1) * half], preferred_element_type=F32
        )
        part[s] = value.astype(BF16)
        if s == 0:
            pl.semaphore_wait(barrier, len(peers))
            tell(1)
        for r in order:
            for dy in (1, 0):
                q = 2 * r + dy
                if q:
                    rs[s, q] = send(
                        part.at[s, piece_of(mp_of(r, dy)), :], part_in.at[s, q],
                        rs_send.at[s, q], rs_recv.at[s, q], {"mp": mp_of(r, dy)},
                    )

    loads[2].wait()
    for b in range(hidden // 128):
        turned[pl.ds(b * 128, 128), :] = grads[:, pl.ds(b * 128, 128)].T
    hear(1)
    tell(2)

    ag = {}
    for s in range(2):
        total = part[s, piece_of(mp), :].astype(F32)
        for q in range(1, 2 * nx):
            rs[s, q].wait()
            total = total + part_in[s, q].astype(F32)
        proj[s, piece_of(mp), :] = total.astype(BF16)
        for r in order:
            for dy in (1, 0):
                q = 2 * r + dy
                if q:
                    ag[s, q] = send(
                        proj.at[s, piece_of(mp), :], proj.at[s, piece_of(mp), :],
                        ag_send.at[s, q], ag_recv.at[s, q], {"mp": mp_of(r, dy)},
                    )
    hear(2)
    tell(3)

    schedule = [[(h, o) for h in HUBS for o in LEAVES[s][h]] for s in range(2)]
    block = rank // 4
    siblings, to_hub = {}, {}

    group = 4

    def multiply(s):
        for b in range(nz // group):
            value = jnp.dot(
                turned[pl.ds(b * group * span, group * span), :], proj[s],
                preferred_element_type=F32,
            ).reshape(group, 2, span // 2, half)
            for c in range(2):
                halves[s, c, pl.ds(b * group, group)] = value[
                    :, :, :, c * block : (c + 1) * block
                ].astype(BF16)
        for n, (h, o) in enumerate(schedule[s]):
            at = (z - o + nz) % nz
            siblings[s, n] = send(
                halves.at[s, 1 - core, at], sibling_in.at[s, n],
                core_send.at[s, n], core_recv.at[s, n], {"dp": dp_of(z, y_hi, 1 - core)},
            )

    def slot(e, dy):
        return (e + 2) * 2 + dy

    def scatter(s, h):
        i = HUBS.index(h)
        members = [n for n in range(nz) if schedule[s][n][0] == h]
        for n in members:
            siblings[s, n].wait()
        for n in members:
            at = (z - schedule[s][n][1] + nz) % nz
            value = halves[s, core, at].astype(F32) + sibling_in[s, n].astype(F32)
            leaf[s, n] = value.astype(BF16)
        for n in members:
            e = schedule[s][n][1] - h
            if h == 0:
                for y in range(2):
                    if e:
                        to_hub[s, 0, e, y] = send(
                            leaf.at[s, n, y], hub_in.at[s, i, slot(e, y)],
                            hub_send.at[s, i, slot(e, y)], hub_recv.at[s, i, slot(e, y)],
                            {"dp": dp_of(z - e + nz, y_hi, core)},
                        )
                continue
            for dy in (1, 0):
                if e or dy:
                    y_at = (y_hi + dy) % 2
                    to_hub[s, h, e, dy] = send(
                        leaf.at[s, n, y_at], hub_in.at[s, i, slot(e, dy)],
                        hub_send.at[s, i, slot(e, dy)], hub_recv.at[s, i, slot(e, dy)],
                        {"dp": dp_of(z - e + nz, y_at, core)},
                    )

    for s in range(2):
        for q in range(1, 2 * nx):
            ag[s, q].wait()
        if s == 1:
            mine = pl.ds(pl.multiple_of(core * (width // 2), width // 2), width // 2)
            far = send(
                basis.at[mine, :], far_basis.at[mine, :], far_send.at[0], far_recv.at[0],
                device_of(2, "row"),
            )
        multiply(s)
        for h in HUBS:
            scatter(s, h)
    hear(3)

    for load in loads[3:]:
        load.wait()
    column[:, pl.ds(span // 2, 8), :] = jnp.zeros((2, 8, block), F32)
    fin = {}
    home = HUBS.index(0)

    def collect(i, h, v, into):
        for s in range(2):
            own = schedule[s].index((h, h))
            value = leaf[s, own, (y_hi + v) % 2].astype(F32)
            for e in [o - h for o in LEAVES[s][h]]:
                for dy in (0, 1):
                    if (e or (dy and h)) and not v:
                        to_hub[s, h, e, dy].wait()
            for e in [o - h for o in LEAVES[s][h]]:
                if h == 0:
                    if e:
                        value = value + hub_in[s, i, slot(e, 0) + (y_hi + v) % 2].astype(F32)
                    continue
                for dy in (0, 1):
                    if e or dy:
                        value = value + hub_in[s, i, slot(e, dy)].astype(F32)
            column[s, pl.ds(0, span // 2), :] = value
            for c in range(2):
                cut = column[s, pl.ds(c * rows, pad), :]
                fin_out[into, c, pl.ds(s * pad, pad), :] = cut.astype(BF16)
        for dc in (1, 0):
            core_at = (core + dc) % 2
            if h or v or dc:
                fin[into, dc] = send(
                    fin_out.at[into, core_at], fin_in.at[into, dc],
                    fin_send.at[into, dc], fin_recv.at[into, dc],
                    {"dp": dp_of(z - h + nz, (y_hi + v) % 2, core_at)},
                )

    for i, h in enumerate(HUBS):
        collect(i, h, 0, i)
        if h == 0:
            collect(i, 0, 1, len(HUBS))

    far.wait()
    swap = send(
        far_basis.at[mine, :], far_basis.at[mine, :], far_send.at[1], far_recv.at[1],
        {"dp": dp_of(z, y_hi, 1 - core)},
    )
    for dc in range(2):
        for i in range(len(HUBS) + 1):
            if i != home or dc:
                fin[i, dc].wait()
        for k in range(2):
            at = pl.ds(k * pad, pad)
            low_grad = (fin_in if dc else fin_out)[home, 1 if dc else core, at, :].astype(F32)
            for i in range(len(HUBS) + 1):
                if i != home:
                    low_grad = low_grad + fin_in[i, dc, at, :].astype(F32)
            low_grad = low_grad[:rows]
            cut = pl.ds(pl.multiple_of((2 * k + (core + dc) % 2) * block, block), block)
            moment_new, second_new = moments(first[:, cut], second[:, cut], low_grad)
            direction = moment_new / corr_one / (jnp.sqrt(second_new / corr_two) + adam_eps)
            grad_out[:, cut] = low_grad
            padded = jnp.concatenate([direction, jnp.zeros((pad - rows, block), F32)], axis=0)
            dirs[0, :, cut] = padded.astype(BF16)

    gathered, returned = {}, {}
    for k in (5, 6, 4, 3, 1, 2):
        gathered[k] = send(
            dirs.at[0], dirs.at[k], dir_send.at[k], dir_recv.at[k], device_of(*HELPERS[k]),
        )

    def update(slots, shard):
        stacked = jnp.concatenate([dirs[k] for k in slots], axis=0)
        product = lax.dot_general(
            stacked, shard[...], (((1,), (1,)), ((), ())), preferred_element_type=F32
        ).astype(BF16)
        return [product[i * pad : (i + 1) * pad] for i in range(len(slots))]

    def give_back(k, value):
        r, via = HELPERS[k]
        blocks[k] = value
        returned[k] = send(
            blocks.at[k], delta.at[k], blk_send.at[k], blk_recv.at[k], device_of(-r, via),
        )

    def apply(r, via, change):
        at = pl.ds(pl.multiple_of(mp_of(r, 0 if via == "row" else 1) * width, width), width)
        change = change.astype(F32)[:rows]
        weights_out[:, at] = (weights[:, at].astype(F32) - step_size * change).astype(BF16)

    near = (5, 6, 3, 1, 2)
    for k in near:
        gathered[k].wait()
    for k, value in zip(near, update(near, basis)):
        give_back(k, value)
    swap.wait()
    gathered[4].wait()
    value, own = update((4, 0), far_basis)
    give_back(4, value)
    apply(2, "row", own)
    apply(0, "row", update((0,), basis)[0])
    for k in (3, 1, 2, 4, 5, 6):
        returned[k].wait()
        r, via = HELPERS[k]
        apply(r + 2 if k == 4 else r, via, delta[k])


def on_device(nz, nx, acts, out_grads, basis, weights, first_moment, second_moment):
    tokens, width = acts.shape
    hidden = out_grads.shape[1]
    rank = basis.shape[1]
    rows, full = weights.shape
    pad = -(-rows // 16) * 16
    span = hidden // nz
    peers = 2 * nx
    piece = tokens // peers
    hubs = len(HUBS)
    arrays = (acts, out_grads, basis, weights, first_moment, second_moment)
    held = [pltpu.with_memory_space_constraint(array, pltpu.HBM) for array in arrays]
    dma = pltpu.SemaphoreType.DMA
    vmem = pltpu.VMEM
    new_weights, low_grad = pl.pallas_call(
        functools.partial(kernel, nz, nx, pad),
        out_shape=(
            jax.ShapeDtypeStruct(weights.shape, BF16),
            jax.ShapeDtypeStruct(first_moment.shape, F32),
        ),
        in_specs=[pl.BlockSpec(memory_space=pltpu.HBM)] * 6,
        out_specs=[pl.BlockSpec(memory_space=pltpu.VMEM)] * 2,
        scratch_shapes=[
            vmem(acts.shape, BF16),
            vmem(out_grads.shape, BF16),
            vmem(basis.shape, BF16),
            vmem(weights.shape, BF16),
            vmem(first_moment.shape, F32),
            vmem(second_moment.shape, F32),
            vmem((2, tokens, rank // 2), BF16),
            vmem((2, peers, piece, rank // 2), BF16),
            vmem((2, tokens, rank // 2), BF16),
            vmem((hidden, tokens), BF16),
            vmem((2, 2, nz, 2, span // 2, rank // 4), BF16),
            vmem((2, nz, 2, span // 2, rank // 4), BF16),
            vmem((2, nz, 2, span // 2, rank // 4), BF16),
            vmem((2, hubs, 10, span // 2, rank // 4), BF16),
            vmem((2, span // 2 + 8, rank // 4), F32),
            vmem((hubs + 1, 2, 2 * pad, rank // 4), BF16),
            vmem((hubs + 1, 2, 2 * pad, rank // 4), BF16),
            vmem((peers, pad, rank), BF16),
            vmem((peers, pad, width), BF16),
            vmem((peers, pad, width), BF16),
            dma((6,)),
            dma((2, peers)), dma((2, peers)), dma((2, peers)), dma((2, peers)),
            dma((2, nz)), dma((2, nz)),
            dma((2, hubs, 10)), dma((2, hubs, 10)), dma((hubs + 1, 2)), dma((hubs + 1, 2)),
            dma((peers,)), dma((peers,)), dma((peers,)), dma((peers,)),
            pltpu.SemaphoreType.REGULAR((3, 2)),
            vmem(basis.shape, BF16),
            dma((2,)), dma((2,)),
        ],
        compiler_params=pltpu.CompilerParams(
            collective_id=0, has_side_effects=True, vmem_limit_bytes=32 * 1024 * 1024
        ),
    )(*held)
    moment_new, second_new = moments(first_moment, second_moment, low_grad)
    return new_weights, moment_new, second_new


def solution(mesh):
    nz, nx = mesh.shape["dp"] // 4, mesh.shape["mp"] // 2
    return jax.shard_map(
        functools.partial(on_device, nz, nx),
        mesh=mesh,
        in_specs=(
            P("dp", "mp"),
            P("dp", "mp"),
            P("mp", None),
            P(("mp", "dp"), None),
            P(("mp", "dp"), None),
            P(("mp", "dp"), None),
        ),
        out_specs=(P(("mp", "dp"), None), P(("mp", "dp"), None), P(("mp", "dp"), None)),
        check_vma=False,
    )
```
